256 devices in a mesh: ctx: 8 (over z), head: 32 (over x, y, core).
Axes of the slice: x: 4, y: 4, z: 8, core: 2. Of those that a mesh axis runs over, the one named last changes fastest.
Arguments:
- queries: bfloat16 [4096, 64, 128], P(('ctx', 'head')), may hold values from -8 to 8, as said below
- keys: bfloat16 [8, 64, 8, 128, 128], P(None, 'head', 'ctx'), may hold values from -4 to 4, as said below
- values: bfloat16 [8, 64, 8, 128, 128], P(None, 'head', 'ctx'), may hold values from -6 to 6
- outputs: bfloat16 [4096, 64, 128], P(('ctx', 'head')), may hold values from -1 to 1
- grad_out: bfloat16 [4096, 64, 128], P(('ctx', 'head')), may hold values from -40 to 40
- block_ids: int32 [32, 8, 48], replicated, may hold values from 0 to 511, as said below
- block_counts: int32 [32, 8], replicated, may hold values from 1 to 48, as said below
Outputs:
- grad_queries: bfloat16 [4096, 64, 128], P(('ctx', 'head'))
- grad_keys: bfloat16 [8, 64, 8, 128, 128], P(None, 'head', 'ctx')
- grad_values: bfloat16 [8, 64, 8, 128, 128], P(None, 'head', 'ctx')
The draws below stay inside these ranges and needn't reach their ends.
Inputs may be any that keep to these rules, and one draw needn't show every extreme that they name: queries are of order one. keys are of order one. block_ids[i, h, 0] = 480 + i, the key block that holds query block i's own positions, and slots from block_counts[i, h] on repeat it; the other live slots hold distinct key blocks before the query slab. Key block g belongs to context group g % 8. The live lists of the query blocks of one context group for one key head name at most 7 distinct blocks of any one group, and in every draw some group and key head name exactly 7 from every group. `block_counts`: some context group has all its lists full for some key head.
All inputs are finite; a program needn't handle non-finite values.
Results may differ from the reference program's by a relative error of at most 0.0049.
Values may be sent and summed in bfloat16 or wider, within the bound.
A program may use at most 128 MiB of HBM per device.

```python
import jax
import jax.numpy as jnp
from jax import lax

HEADS = 64
KV_HEADS = 8
DH = 128
BLK = 128
NSEL = 48
QB_G = 4
QBLK = 32
QT = 4096
BPG = 64
KBLK = 512
CAP = 7
N_CTX = 8


def draw_queries(key, part):
    own_key = jax.random.fold_in(key, 1)
    shape_q = (QT, HEADS, DH)
    drawn = jax.random.truncated_normal(own_key, -4.0, 4.0, shape_q, jnp.float32)
    return drawn.astype(jnp.bfloat16)


def draw_keys(key, part):
    own_key = jax.random.fold_in(key, 2)
    shape_k = (KV_HEADS, BPG, N_CTX, BLK, DH)
    drawn = jax.random.truncated_normal(own_key, -4.0, 4.0, shape_k, jnp.float32)
    return drawn.astype(jnp.bfloat16)


def make_lists(key):
    base_key = jax.random.fold_in(key, 11)
    pre_count = (KBLK - QBLK) // N_CTX
    pool_len = N_CTX * CAP - QB_G
    full_group = jax.random.randint(jax.random.fold_in(base_key, 1), (), 0, N_CTX)
    full_head = jax.random.randint(jax.random.fold_in(base_key, 2), (), 0, KV_HEADS)

    def one_list(dest, head_id):
        pair_key = jax.random.fold_in(jax.random.fold_in(base_key, 100 + dest), head_id)
        src_keys = jax.random.split(pair_key, N_CTX)
        drawn_loc = jax.vmap(lambda src_key: jax.random.permutation(src_key, pre_count)[:CAP])(src_keys)
        query_ids = dest * QB_G + jnp.arange(QB_G)
        diag_count = jnp.sum((query_ids[None, :] % N_CTX == jnp.arange(N_CTX)[:, None]).astype(jnp.int32), axis=1)
        keep_it = jnp.arange(CAP)[None, :] < (CAP - diag_count)[:, None]
        global_ids = drawn_loc * N_CTX + jnp.arange(N_CTX)[:, None]
        ordering = jnp.argsort(jnp.where(keep_it.reshape(-1), 0, N_CTX * CAP) + jnp.arange(N_CTX * CAP))
        pool_ids = global_ids.reshape(-1)[ordering[:pool_len]]
        pool_ids = jax.random.permutation(jax.random.fold_in(pair_key, 7), pool_ids)
        pick_at = (jnp.arange(QB_G)[:, None] * (NSEL - 1) + jnp.arange(NSEL - 1)[None, :]) % pool_len
        diag_ids = KBLK - QBLK + query_ids
        return jnp.concatenate([diag_ids[:, None], pool_ids[pick_at]], axis=1)
    block_lists = jax.vmap(lambda dest: jax.vmap(lambda head_id: one_list(dest, head_id))(jnp.arange(KV_HEADS)))(jnp.arange(N_CTX))
    block_lists = jnp.transpose(block_lists, (0, 2, 1, 3)).reshape(QBLK, KV_HEADS, NSEL)
    shift_by = jax.random.randint(jax.random.fold_in(base_key, 3), (N_CTX,), 0, 3)
    high_count = NSEL // jnp.left_shift(1, shift_by)
    low_count = jnp.maximum(high_count // 2, 1)
    counts = jax.random.randint(jax.random.fold_in(base_key, 4), (N_CTX, QB_G, KV_HEADS), low_count[:, None, None], high_count[:, None, None] + 1)
    is_full = (jnp.arange(N_CTX)[:, None, None] == full_group) & (jnp.arange(KV_HEADS)[None, None, :] == full_head)
    counts = jnp.where(is_full, NSEL, counts).reshape(QBLK, KV_HEADS)
    slot_num = jnp.arange(NSEL)
    block_lists = jnp.where(slot_num[None, None, :] < counts[:, :, None], block_lists, block_lists[:, :, :1])
    return (block_lists.astype(jnp.int32), counts.astype(jnp.int32))


def draw_block_ids(key, part):
    return make_lists(key)[0]


def draw_block_counts(key, part):
    return make_lists(key)[1]


def block_scale(key, dims, cuts, least, high):
    def one(axis_at, shards_of):
        steps = jax.random.uniform(jax.random.fold_in(jax.random.fold_in(key, 6), axis_at), (shards_of,), jnp.float32, least / len(cuts), high / len(cuts))
        return jnp.repeat(jnp.exp(steps), dims[axis_at] // shards_of).reshape((-1,) + (1,) * (len(dims) - axis_at - 1))

    gain = one(*cuts[0])
    for cut in cuts[1:]:
        gain = gain * one(*cut)
    return gain


def gaussian(key, extent, scale, limit, cuts=(), held_as=jnp.bfloat16):
    array = jax.random.normal(key, extent, jnp.float32) * scale
    if len(cuts) > 0:
        array = block_scale(key, extent, cuts, -0.22, 0.18) * array
    return jnp.clip(array, min=-limit, max=limit).astype(held_as)


def setup_inputs(seed: int = 0) -> dict:
    seeds = jax.random.split(jax.random.key(seed), 8)
    queries = draw_queries(jax.random.fold_in(seeds[7], 71), 0)
    keys = draw_keys(jax.random.fold_in(seeds[7], 71), 0)
    values = gaussian(seeds[2], (KV_HEADS, BPG, N_CTX, BLK, DH), 1.0, 6.0, ((1, 32), (2, 8)))
    outputs = jnp.clip(jax.random.uniform(seeds[3], (QT, HEADS, DH), jnp.float32, -1.0, 1.0) * block_scale(seeds[3], (QT, HEADS, DH), ((0, 256),), -0.4, 0.0), -1.0, 1.0).astype(jnp.bfloat16)
    grad_out = jnp.clip(jax.random.uniform(seeds[4], (QT, HEADS, DH), jnp.float32, -40.0, 40.0) * block_scale(seeds[4], (QT, HEADS, DH), ((0, 256),), -0.4, 0.0), -40.0, 40.0).astype(jnp.bfloat16)
    block_ids = draw_block_ids(jax.random.fold_in(seeds[7], 71), 0)
    block_counts = draw_block_counts(jax.random.fold_in(seeds[7], 71), 0)
    return {"queries": queries, "keys": keys, "values": values, "outputs": outputs, "grad_out": grad_out, "block_ids": block_ids, "block_counts": block_counts}


neg_fill = -1e30


def pick_rows(stored, wanted):
    return stored[wanted]


def reference(queries, keys, values, outputs, grad_out, block_ids, block_counts):
    group_size = HEADS // KV_HEADS
    scaling = DH ** -0.5
    key_blocks = keys.reshape(KV_HEADS, KBLK, BLK, DH)
    value_blocks = values.reshape(KV_HEADS, KBLK, BLK, DH)
    query_rows = queries.reshape(QBLK, BLK, KV_HEADS, group_size, DH)
    grad_rows = grad_out.reshape(QBLK, BLK, KV_HEADS, group_size, DH)
    delta = jnp.sum(grad_out.astype(jnp.float32) * outputs.astype(jnp.float32), axis=-1)
    delta = delta.reshape(QBLK, BLK, KV_HEADS, group_size)
    slot_of = jnp.arange(NSEL * BLK, dtype=jnp.int32) // BLK
    offset = jnp.arange(NSEL * BLK, dtype=jnp.int32) % BLK
    head_rows = jnp.arange(KV_HEADS, dtype=jnp.int32)[:, None]

    def one_block(carried, item):
        grad_keys, grad_values = carried
        number, query_blk, grad_blk, delta_blk, chosen, live_count = item
        picked_keys = jax.vmap(pick_rows)(key_blocks, chosen).reshape(KV_HEADS, NSEL * BLK, DH)
        picked_values = jax.vmap(pick_rows)(value_blocks, chosen).reshape(KV_HEADS, NSEL * BLK, DH)
        score = jnp.einsum('qhgd,hkd->hgqk', query_blk.astype(jnp.float32), picked_keys.astype(jnp.float32)) * scaling
        key_pos = chosen[:, slot_of] * BLK + offset[None, :]
        query_pos = (KBLK - QBLK + number) * BLK + jnp.arange(BLK, dtype=jnp.int32)
        allowed = (slot_of[None, :] < live_count[:, None])[:, None, :] & (key_pos[:, None, :] <= query_pos[None, :, None])
        allowed = allowed[:, None]
        top = jnp.max(jnp.where(allowed, score, neg_fill), axis=-1, keepdims=True)
        weight = jnp.where(allowed, jnp.exp(score - top), 0.0)
        prob = weight / jnp.sum(weight, axis=-1, keepdims=True)
        prob_low = prob.astype(jnp.bfloat16)
        dprob = jnp.einsum('qhgd,hkd->hgqk', grad_blk.astype(jnp.float32), picked_values.astype(jnp.float32))
        delta_heads = jnp.transpose(delta_blk, (1, 2, 0))
        dscore = (prob * (dprob - delta_heads[..., None])).astype(jnp.bfloat16)
        grad_q = jnp.einsum('hgqk,hkd->qhgd', dscore.astype(jnp.float32), picked_keys.astype(jnp.float32)) * scaling
        part_k = jnp.einsum('hgqk,qhgd->hkd', dscore.astype(jnp.float32), query_blk.astype(jnp.float32)) * scaling
        part_v = jnp.einsum('hgqk,qhgd->hkd', prob_low.astype(jnp.float32), grad_blk.astype(jnp.float32))
        grad_keys = grad_keys.at[head_rows, chosen].add(part_k.reshape(KV_HEADS, NSEL, BLK, DH))
        grad_values = grad_values.at[head_rows, chosen].add(part_v.reshape(KV_HEADS, NSEL, BLK, DH))
        return (grad_keys, grad_values), grad_q.astype(jnp.bfloat16)

    start = (jnp.zeros((KV_HEADS, KBLK, BLK, DH), jnp.float32), jnp.zeros((KV_HEADS, KBLK, BLK, DH), jnp.float32))
    items = (jnp.arange(QBLK, dtype=jnp.int32), query_rows, grad_rows, delta, block_ids, block_counts)
    (grad_keys, grad_values), grad_q = lax.scan(one_block, start, items)
    grad_queries = grad_q.reshape(QT, HEADS, DH)
    grad_keys = grad_keys.reshape(KV_HEADS, BPG, N_CTX, BLK, DH).astype(jnp.bfloat16)
    grad_values = grad_values.reshape(KV_HEADS, BPG, N_CTX, BLK, DH).astype(jnp.bfloat16)
    return grad_queries, grad_keys, grad_values
```

```python
import functools

import jax
import jax.numpy as jnp
from jax import lax
from jax.experimental import pallas as pl
from jax.experimental.pallas import tpu as pltpu
from jax.sharding import PartitionSpec as P

MESH = pl.DeviceIdType.MESH
VMEM = pltpu.VMEM
SMEM = pltpu.SMEM
NEG = -1e30
LOG2E = 1.4426950408889634
LANES = 128
FAR = 4096


def whole(space):
    return pl.BlockSpec(memory_space=space)


def nt(a, b):
    return lax.dot_general(a, b, (((1,), (1,)), ((), ())), preferred_element_type=jnp.float32)


def nn(a, b):
    return lax.dot_general(a, b, (((1,), (0,)), ((), ())), preferred_element_type=jnp.float32)


def iota(shape, dim):
    return lax.broadcasted_iota(jnp.int32, shape, dim)


def plan_kernel(dims, lists_ref, counts_ref, ids_ref, thr_ref, inv_ref):
    n_ctx, members, per_group, own, cap = dims
    g = lax.axis_index("ctx")
    h = lax.axis_index("head") // members
    blocks, kv, slots = lists_ref.shape
    total = n_ctx * per_group
    pick = iota((blocks, kv, slots), 1) == h
    lists = jnp.sum(jnp.where(pick, lists_ref[...].astype(jnp.float32), 0.0), axis=1)
    count = jnp.sum(
        jnp.where(iota((blocks, kv), 1) == h, counts_ref[...].astype(jnp.float32), 0.0),
        axis=1,
        keepdims=True,
    )
    lists = jnp.where(iota((blocks, slots), 1).astype(jnp.float32) < count, lists, -1.0)
    col = iota((1, total), 1)
    col_id = ((col % per_group) * n_ctx + col // per_group).astype(jnp.float32)
    live = jnp.zeros((blocks, total), jnp.float32)
    for n in range(slots):
        live = jnp.where(lists[:, n : n + 1] == col_id, 1.0, live)
    low = live.astype(jnp.bfloat16)
    of_group = (iota((8, blocks), 1) // own == iota((8, blocks), 0)).astype(jnp.float32)
    used = nn(of_group.astype(jnp.bfloat16), low) > 0.5
    used_f = used.astype(jnp.float32)
    before = (iota((total, total), 0) // per_group == iota((total, total), 1) // per_group) & (
        iota((total, total), 0) < iota((total, total), 1)
    )
    place = nn(used_f.astype(jnp.bfloat16), before.astype(jnp.float32).astype(jnp.bfloat16))
    rows8 = iota((8, blocks), 0)
    own_rows = ((iota((8, blocks), 1) == own * g + rows8) & (rows8 < own)).astype(jnp.float32)
    own_live = nn(own_rows.astype(jnp.bfloat16), low)
    row8 = iota((8, total), 0)
    diag = (
        (col_id == (total - blocks + own * g + row8).astype(jnp.float32)) & (row8 < own)
    ).astype(jnp.float32)
    key_row = iota((total, 2 * LANES), 0)
    lane = iota((total, 2 * LANES), 1)
    key_group = key_row // per_group
    key_local = key_row % per_group
    got = jnp.zeros((24, 2 * LANES), jnp.float32)
    for k in range(cap):
        match = jnp.where(used & (place == k), 1.0, 0.0)
        mine = jnp.sum(jnp.where(row8 == g, match, 0.0), axis=0, keepdims=True)
        left = jnp.concatenate([match, own_live * mine, diag * mine], axis=0)
        right = jnp.where(
            lane == k,
            jnp.where(key_group == g, key_local, 0),
            jnp.where(lane == LANES + k * n_ctx + key_group, 1, 0),
        )
        got = got + nn(left.astype(jnp.bfloat16), right.astype(jnp.float32).astype(jnp.bfloat16))
    ids_ref[...] = got[0:8, :LANES].astype(jnp.int32)
    is_live = got[8:16, LANES:] > 0.5
    is_diag = got[16:24, LANES:] > 0.5
    thr_ref[...] = jnp.where(is_diag & is_live, 0, jnp.where(is_live, -FAR, FAR))
    held_at = ((iota((total, LANES), 0) // per_group == g)
               & (iota((total, LANES), 0) % per_group == iota((total, LANES), 1)))
    back = nn(
        jnp.where(used, place, float(cap)).astype(jnp.bfloat16),
        held_at.astype(jnp.float32).astype(jnp.bfloat16),
    )
    inv_ref[...] = back.astype(jnp.int32)


def greet(g, d, n_ctx, n_head):
    barrier = pltpu.get_barrier_semaphore()

    def plane(o, _):
        pl.semaphore_signal(
            barrier, inc=1, device_id=(g, lax.rem(d + o, n_head)), device_id_type=MESH
        )
        return 0

    lax.fori_loop(1, n_head, plane, 0)

    def line(o, _):
        pl.semaphore_signal(
            barrier, inc=1, device_id=(lax.rem(g + o, n_ctx), d), device_id_type=MESH
        )
        return 0

    lax.fori_loop(1, n_ctx, line, 0)
    pl.semaphore_wait(barrier, n_head + n_ctx - 2)


def await_bytes(ref, sem):
    pltpu.make_async_copy(ref, ref, sem).wait()


def spread_kernel(
    dims,
    ids,
    q,
    do,
    dl,
    keys,
    vals,
    k_got,
    v_got,
    q_got,
    do_got,
    dl_got,
    k_held,
    v_held,
    k_send,
    v_send,
    ss,
    rs,
):
    n_ctx, n_head, members, per_dev, quarter, cap = dims
    g = lax.axis_index("ctx")
    d = lax.axis_index("head")
    greet(g, d, n_ctx, n_head)

    def held_pair(src, p, held):
        return (
            src.at[p // members, :, 0, pl.ds((p % members) * quarter, quarter), :],
            held.at[pl.ds(per_dev * d, per_dev)],
        )

    def send(src, dst, n, to):
        pltpu.make_async_remote_copy(
            src_ref=src,
            dst_ref=dst,
            send_sem=ss.at[n],
            recv_sem=rs.at[n],
            device_id=to,
            device_id_type=MESH,
        ).start()

    def send_kv(o, _):
        p = lax.rem(d + o, n_head)
        send(*held_pair(keys, p, k_held), 0, (g, p))
        send(*held_pair(vals, p, v_held), 1, (g, p))
        return 0

    lax.fori_loop(1, n_head, send_kv, 0)
    pltpu.make_async_copy(*held_pair(keys, d, k_held), rs.at[0]).start()
    pltpu.make_async_copy(*held_pair(vals, d, v_held), rs.at[1]).start()

    def send_q(o, _):
        p = lax.rem(d + o, n_head)
        h = p // members
        send(q.at[h], q_got.at[d], 2, (g, p))
        send(do.at[h], do_got.at[d], 3, (g, p))
        send(dl.at[h], dl_got.at[d], 4, (g, p))
        return 0

    lax.fori_loop(1, n_head, send_q, 0)
    h = d // members
    pltpu.make_async_copy(q.at[h], q_got.at[d], rs.at[2]).start()
    pltpu.make_async_copy(do.at[h], do_got.at[d], rs.at[3]).start()
    pltpu.make_async_copy(dl.at[h], dl_got.at[d], rs.at[4]).start()

    for n, held, packed, out in ((0, k_held, k_send, k_got), (1, v_held, v_send, v_got)):
        await_bytes(held, rs.at[n])

        def pack(c, _, held=held, packed=packed):
            for k in range(cap):
                packed[c, k] = held[ids[c, k]]
            return 0

        lax.fori_loop(0, n_ctx, pack, 0)

        def send_line(o, _, packed=packed, out=out, n=n):
            c = lax.rem(g + o, n_ctx)
            send(packed.at[c], out.at[g], 5 + n, (c, d))
            return 0

        lax.fori_loop(1, n_ctx, send_line, 0)
        pltpu.make_async_copy(packed.at[g], out.at[g], rs.at[5 + n]).start()

    for n, ref in ((2, q_got), (3, do_got), (4, dl_got), (5, k_got), (6, v_got)):
        await_bytes(ref, rs.at[n])
    for n, ref in ((0, k_held), (1, v_held)):
        await_bytes(ref.at[pl.ds(0, per_dev * (n_head - 1))], ss.at[n])
    for n, ref in ((2, q_got), (3, do_got), (4, dl_got)):
        await_bytes(ref.at[pl.ds(0, n_head - 1)], ss.at[n])
    for n, ref in ((5, k_got), (6, v_got)):
        await_bytes(ref.at[pl.ds(0, n_ctx - 1)], ss.at[n])


def share_kernel(dims, stats, got, ss, rs):
    members = dims
    g = lax.axis_index("ctx")
    d = lax.axis_index("head")
    first = (d // members) * members
    me = d % members
    barrier = pltpu.get_barrier_semaphore()
    for o in range(1, members):
        pl.semaphore_signal(
            barrier, inc=1, device_id=(g, first + lax.rem(me + o, members)), device_id_type=MESH
        )
    pl.semaphore_wait(barrier, members - 1)
    for o in range(1, members):
        pltpu.make_async_remote_copy(
            src_ref=stats,
            dst_ref=got.at[me],
            send_sem=ss,
            recv_sem=rs,
            device_id=(g, first + lax.rem(me + o, members)),
            device_id_type=MESH,
        ).start()
    pltpu.make_async_copy(stats, got.at[me], rs).start()
    await_bytes(got, rs)
    await_bytes(got.at[pl.ds(0, members - 1)], ss)


def gather_kernel(
    dims,
    inv,
    gq,
    gk,
    gv,
    gq_out,
    gk_out,
    gv_out,
    gq_got,
    k_back,
    v_back,
    k_sum,
    v_sum,
    ss,
    rs,
):
    n_ctx, n_head, members, per_dev, quarter, cap = dims
    g = lax.axis_index("ctx")
    d = lax.axis_index("head")
    h = d // members
    m = d % members
    greet(g, d, n_ctx, n_head)

    def send(src, dst, n, to):
        pltpu.make_async_remote_copy(
            src_ref=src,
            dst_ref=dst,
            send_sem=ss.at[n],
            recv_sem=rs.at[n],
            device_id=to,
            device_id_type=MESH,
        ).start()

    for n, src, back in ((0, gk, k_back), (1, gv, v_back)):

        def send_line(o, _, src=src, back=back, n=n):
            c = lax.rem(g + o, n_ctx)
            send(src.at[c], back.at[g, pl.ds(0, cap)], n, (c, d))
            return 0

        lax.fori_loop(1, n_ctx, send_line, 0)
        pltpu.make_async_copy(src.at[g], back.at[g, pl.ds(0, cap)], rs.at[n]).start()

    def send_q(o, _):
        p = lax.rem(d + o, n_head)
        send(gq.at[p], gq_got.at[d], 2, (g, p))
        return 0

    lax.fori_loop(1, n_head, send_q, 0)
    pltpu.make_async_copy(gq.at[d], gq_got.at[d], rs.at[2]).start()

    for n, src, back, total, out in (
        (0, gk, k_back, k_sum, gk_out),
        (1, gv, v_back, v_sum, gv_out),
    ):
        for c in range(n_ctx):
            back[c, cap] = jnp.zeros(back.shape[2:], back.dtype)
        await_bytes(src, rs.at[n])

        def add_up(l, _, back=back, total=total):
            acc = back[0, inv[0, l]].astype(jnp.float32)
            for c in range(1, n_ctx):
                acc = acc + back[c, inv[c, l]].astype(jnp.float32)
            total[l] = acc.astype(total.dtype)
            return 0

        lax.fori_loop(0, per_dev * n_head, add_up, 0)

        def place(out=out):
            return out.at[h, :, 0, pl.ds(m * quarter, quarter), :]

        def send_home(o, _, total=total, n=n, place=place):
            p = lax.rem(d + o, n_head)
            send(total.at[pl.ds(per_dev * p, per_dev)], place(), 3 + n, (g, p))
            return 0

        lax.fori_loop(1, n_head, send_home, 0)
        pltpu.make_async_copy(total.at[pl.ds(per_dev * d, per_dev)], place(), rs.at[3 + n]).start()

    await_bytes(gq_got, rs.at[2])

    def add_q(e, _):
        acc = gq_got[members * e].astype(jnp.float32)
        for o in range(1, members):
            acc = acc + gq_got[members * e + o].astype(jnp.float32)
        gq_out[e] = acc.astype(gq_out.dtype)
        return 0

    lax.fori_loop(0, n_head // members, add_q, 0)
    await_bytes(k_sum, rs.at[3])
    await_bytes(v_sum, rs.at[4])
    for n, ref in ((0, gk), (1, gv)):
        await_bytes(ref.at[pl.ds(0, n_ctx - 1)], ss.at[n])
    await_bytes(gq.at[pl.ds(0, n_head - 1)], ss.at[2])
    for n, ref in ((3, k_sum), (4, v_sum)):
        await_bytes(ref.at[pl.ds(0, per_dev * (n_head - 1))], ss.at[n])


def reach(rows, quarter, m):
    shape = (quarter, rows)
    return iota(shape, 1) // 8 - iota(shape, 0) - m * quarter


def scaled(thr, i, c, n_ctx, cap, quarter, gap, raw):
    factor = (LANES ** -0.5) * LOG2E
    parts = []
    for k in range(cap):
        part = raw[k * quarter : (k + 1) * quarter] * factor
        parts.append(jnp.where(gap >= thr[i, k * n_ctx + c], part, NEG))
    return jnp.concatenate(parts, axis=0)


def stats_kernel(dims, thr, k_got, q_got, stats):
    n_ctx, members, quarter, cap, own, rows = dims
    m = lax.axis_index("head") % members
    gap = reach(rows, quarter, m)

    def one(i, _):
        def step(c, carry):
            top, mass = carry
            raw = nt(k_got[pl.ds(c * cap * quarter, cap * quarter)], q_got[pl.ds(i * rows, rows)])
            score = scaled(thr, i, c, n_ctx, cap, quarter, gap, raw)
            new = jnp.maximum(top, jnp.max(score, axis=0, keepdims=True))
            mass = mass * jnp.exp2(top - new) + jnp.sum(
                jnp.exp2(score - new), axis=0, keepdims=True
            )
            return new, mass

        top, mass = lax.fori_loop(
            0,
            n_ctx,
            step,
            (jnp.full((1, rows), NEG, jnp.float32), jnp.zeros((1, rows), jnp.float32)),
        )
        stats[pl.ds(i, 1)] = top
        stats[pl.ds(4 + i, 1)] = mass
        return 0

    lax.fori_loop(0, own, one, 0)


def grads_kernel(dims, thr, shared, dl_got, k_got, v_got, q_got, do_got, gq, gk, gv, lse, delta, gq_t):
    n_ctx, members, quarter, cap, own, rows = dims
    m = lax.axis_index("head") % members
    gap = reach(rows, quarter, m)
    c = pl.program_id(0)
    scaling = LANES ** -0.5

    @pl.when(c == 0)
    def _():
        gq_t[...] = jnp.zeros_like(gq_t)
        for i in range(own):
            tops = [shared[e, i : i + 1] for e in range(members)]
            top = functools.reduce(jnp.maximum, tops)
            mass = sum(shared[e, 4 + i : 5 + i] * jnp.exp2(tops[e] - top) for e in range(members))
            lse[i : i + 1] = top + jnp.log2(mass)
            per = rows // LANES
            delta[i : i + 1] = jnp.concatenate([dl_got[i * per + e] for e in range(per)], axis=1)

    keys = k_got[0]
    vals = v_got[0]
    keys_t = keys.T

    def one(i, carry):
        acc_k, acc_v = carry
        q = q_got[pl.ds(i * rows, rows)]
        do = do_got[pl.ds(i * rows, rows)]
        score = scaled(thr, i, c, n_ctx, cap, quarter, gap, nt(keys, q))
        prob = jnp.exp2(score - lse[pl.ds(i, 1)])
        dprob = nt(vals, do)
        dscore = (prob * (dprob - delta[pl.ds(i, 1)])).astype(jnp.bfloat16)
        acc_v = acc_v + nn(prob.astype(jnp.bfloat16), do)
        acc_k = acc_k + nn(dscore, q)
        gq_t[i] += nn(keys_t, dscore)
        return acc_k, acc_v

    zero = jnp.zeros((cap * quarter, LANES), jnp.float32)
    acc_k, acc_v = lax.fori_loop(0, own, one, (zero, zero))
    gk[0] = (acc_k * scaling).astype(gk.dtype)
    gv[0] = acc_v.astype(gv.dtype)

    @pl.when(c == n_ctx - 1)
    def _():
        for i in range(own):
            gq[i * rows : (i + 1) * rows] = (gq_t[i].T * scaling).astype(gq.dtype)


def body(queries, keys, values, outputs, grad_out, block_ids, block_counts):
    f32, bf16, i32 = jnp.float32, jnp.bfloat16, jnp.int32
    n_ctx = lax.axis_size("ctx")
    n_head = lax.axis_size("head")
    kv, per_dev, _, blk, dh = keys.shape
    tokens, heads, _ = queries.shape
    members = n_head // kv
    quarter = blk // members
    group = heads // kv
    per_group = per_dev * n_head
    blocks, _, slots = block_ids.shape
    own = blocks // n_ctx
    cap = (slots + own + n_ctx - 2) // n_ctx
    part = tokens * group
    rows = blk * group
    any_ = whole(pl.ANY)
    vm = whole(VMEM)
    sm = whole(SMEM)
    limit = 60 * 2**20

    def by_kv(x):
        return jnp.transpose(x.reshape(tokens, kv, group, dh), (1, 0, 2, 3)).reshape(kv, part, dh)

    delta = jnp.sum(grad_out.astype(f32) * outputs.astype(f32), axis=2)
    delta = jnp.transpose(delta.reshape(tokens, kv, group), (1, 0, 2)).reshape(kv, 1, part)
    q8 = by_kv(queries)
    do8 = by_kv(grad_out)

    ids, thr, inv = pl.pallas_call(
        functools.partial(plan_kernel, (n_ctx, members, per_group, own, cap)),
        out_shape=[jax.ShapeDtypeStruct((8, LANES), i32)] * 3,
        in_specs=[vm, vm],
        out_specs=[vm] * 3,
        compiler_params=pltpu.CompilerParams(vmem_limit_bytes=limit),
        name="plan",
    )(block_ids, block_counts)

    comm = (n_ctx, n_head, members, per_dev, quarter, cap)
    packed = (n_ctx, cap, quarter, dh)
    held = (per_group, quarter, dh)
    k_got, v_got, q_got, do_got, dl_got = pl.pallas_call(
        functools.partial(spread_kernel, comm),
        out_shape=[
            jax.ShapeDtypeStruct(packed, bf16),
            jax.ShapeDtypeStruct(packed, bf16),
            jax.ShapeDtypeStruct((n_head, part, dh), bf16),
            jax.ShapeDtypeStruct((n_head, part, dh), bf16),
            jax.ShapeDtypeStruct((n_head, 1, part), f32),
        ],
        in_specs=[sm] + [any_] * 5,
        out_specs=[any_] * 5,
        scratch_shapes=[
            VMEM(held, bf16),
            VMEM(held, bf16),
            VMEM(packed, bf16),
            VMEM(packed, bf16),
            pltpu.SemaphoreType.DMA((7,)),
            pltpu.SemaphoreType.DMA((7,)),
        ],
        compiler_params=pltpu.CompilerParams(
            collective_id=0, has_side_effects=True, vmem_limit_bytes=16 * 2**20
        ),
        name="spread",
    )(ids, q8, do8, delta, keys, values)

    comp = (n_ctx, members, quarter, cap, own, rows)
    keys_own = k_got.reshape(n_ctx * cap * quarter, dh)
    q_rows = q_got.reshape(n_head * part, dh)
    do_rows = do_got.reshape(n_head * part, dh)
    stats = pl.pallas_call(
        functools.partial(stats_kernel, comp),
        out_shape=jax.ShapeDtypeStruct((8, rows), f32),
        in_specs=[sm, vm, vm],
        out_specs=vm,
        compiler_params=pltpu.CompilerParams(vmem_limit_bytes=limit),
        name="stats",
    )(thr, keys_own, q_rows)

    shared = pl.pallas_call(
        functools.partial(share_kernel, members),
        out_shape=jax.ShapeDtypeStruct((members, 8, rows), f32),
        in_specs=[vm],
        out_specs=vm,
        scratch_shapes=[pltpu.SemaphoreType.DMA, pltpu.SemaphoreType.DMA],
        compiler_params=pltpu.CompilerParams(
            collective_id=1, has_side_effects=True, vmem_limit_bytes=16 * 2**20
        ),
        name="share",
    )(stats)

    chunk = (n_ctx, cap * quarter, dh)
    block = pl.BlockSpec((1, cap * quarter, dh), lambda c: (c, 0, 0))
    gq, gk, gv = pl.pallas_call(
        functools.partial(grads_kernel, comp),
        grid=(n_ctx,),
        out_shape=[
            jax.ShapeDtypeStruct((n_head * part, dh), bf16),
            jax.ShapeDtypeStruct(chunk, bf16),
            jax.ShapeDtypeStruct(chunk, bf16),
        ],
        in_specs=[sm, vm, vm, block, block, vm, vm],
        out_specs=[vm, block, block],
        scratch_shapes=[
            VMEM((own, rows), f32),
            VMEM((own, rows), f32),
            VMEM((own, dh, rows), f32),
        ],
        compiler_params=pltpu.CompilerParams(vmem_limit_bytes=limit),
        name="grads",
    )(thr, shared, dl_got, k_got.reshape(chunk), v_got.reshape(chunk), q_rows, do_rows)

    back = (n_ctx, cap + 1, quarter, dh)
    gq8, grad_keys, grad_values = pl.pallas_call(
        functools.partial(gather_kernel, comm),
        out_shape=[
            jax.ShapeDtypeStruct((kv, part, dh), bf16),
            jax.ShapeDtypeStruct(keys.shape, bf16),
            jax.ShapeDtypeStruct(keys.shape, bf16),
        ],
        in_specs=[sm, any_, any_, any_],
        out_specs=[vm, any_, any_],
        scratch_shapes=[
            VMEM((n_head, part, dh), bf16),
            VMEM(back, bf16),
            VMEM(back, bf16),
            VMEM(held, bf16),
            VMEM(held, bf16),
            pltpu.SemaphoreType.DMA((5,)),
            pltpu.SemaphoreType.DMA((5,)),
        ],
        compiler_params=pltpu.CompilerParams(
            collective_id=2, has_side_effects=True, vmem_limit_bytes=16 * 2**20
        ),
        name="gather",
    )(inv, gq.reshape(n_head, part, dh), gk.reshape(packed), gv.reshape(packed))
    grad_queries = jnp.transpose(gq8.reshape(kv, tokens, group, dh), (1, 0, 2, 3)).reshape(
        tokens, heads, dh
    )
    return grad_queries, grad_keys, grad_values


def solution(mesh):
    tok = P(("ctx", "head"), None, None)
    cached = P(None, "head", "ctx", None, None)
    return jax.shard_map(
        body,
        mesh=mesh,
        in_specs=(tok, cached, cached, tok, tok, P(), P()),
        out_specs=(tok, cached, cached),
        check_vma=False,
    )
```

```python
import functools

import jax
import jax.numpy as jnp
from jax import lax
from jax.experimental import pallas as pl
from jax.experimental.pallas import tpu as pltpu
from jax.sharding import PartitionSpec as P

MESH = pl.DeviceIdType.MESH
VMEM = pltpu.VMEM
SMEM = pltpu.SMEM
NEG = -1e30
LOG2E = 1.4426950408889634
LANES = 128
FAR = 4096


def whole(space):
    return pl.BlockSpec(memory_space=space)


def nt(a, b):
    return lax.dot_general(a, b, (((1,), (1,)), ((), ())), preferred_element_type=jnp.float32)


def nn(a, b):
    return lax.dot_general(a, b, (((1,), (0,)), ((), ())), preferred_element_type=jnp.float32)


def iota(shape, dim):
    return lax.broadcasted_iota(jnp.int32, shape, dim)


def plan_kernel(dims, lists_ref, counts_ref, ids_ref, thr_ref, inv_ref):
    n_ctx, members, per_group, own, cap = dims
    g = lax.axis_index("ctx")
    h = lax.axis_index("head") // members
    blocks, kv, slots = lists_ref.shape
    total = n_ctx * per_group
    pick = iota((blocks, kv, slots), 1) == h
    lists = jnp.sum(jnp.where(pick, lists_ref[...].astype(jnp.float32), 0.0), axis=1)
    count = jnp.sum(
        jnp.where(iota((blocks, kv), 1) == h, counts_ref[...].astype(jnp.float32), 0.0),
        axis=1,
        keepdims=True,
    )
    lists = jnp.where(iota((blocks, slots), 1).astype(jnp.float32) < count, lists, -1.0)
    col = iota((1, total), 1)
    col_id = ((col % per_group) * n_ctx + col // per_group).astype(jnp.float32)
    live = jnp.zeros((blocks, total), jnp.float32)
    for n in range(slots):
        live = jnp.where(lists[:, n : n + 1] == col_id, 1.0, live)
    low = live.astype(jnp.bfloat16)
    of_group = (iota((8, blocks), 1) // own == iota((8, blocks), 0)).astype(jnp.float32)
    used = nn(of_group.astype(jnp.bfloat16), low) > 0.5
    used_f = used.astype(jnp.float32)
    before = (iota((total, total), 0) // per_group == iota((total, total), 1) // per_group) & (
        iota((total, total), 0) < iota((total, total), 1)
    )
    place = nn(used_f.astype(jnp.bfloat16), before.astype(jnp.float32).astype(jnp.bfloat16))
    rows8 = iota((8, blocks), 0)
    own_rows = ((iota((8, blocks), 1) == own * g + rows8) & (rows8 < own)).astype(jnp.float32)
    own_live = nn(own_rows.astype(jnp.bfloat16), low)
    row8 = iota((8, total), 0)
    diag = (
        (col_id == (total - blocks + own * g + row8).astype(jnp.float32)) & (row8 < own)
    ).astype(jnp.float32)
    key_row = iota((total, 2 * LANES), 0)
    lane = iota((total, 2 * LANES), 1)
    key_group = key_row // per_group
    key_local = key_row % per_group
    got = jnp.zeros((24, 2 * LANES), jnp.float32)
    for k in range(cap):
        match = jnp.where(used & (place == k), 1.0, 0.0)
        mine = jnp.sum(jnp.where(row8 == g, match, 0.0), axis=0, keepdims=True)
        left = jnp.concatenate([match, own_live * mine, diag * mine], axis=0)
        right = jnp.where(
            lane == k,
            jnp.where(key_group == g, key_local, 0),
            jnp.where(lane == LANES + k * n_ctx + key_group, 1, 0),
        )
        got = got + nn(left.astype(jnp.bfloat16), right.astype(jnp.float32).astype(jnp.bfloat16))
    ids_ref[...] = got[0:8, :LANES].astype(jnp.int32)
    is_live = got[8:16, LANES:] > 0.5
    is_diag = got[16:24, LANES:] > 0.5
    thr_ref[...] = jnp.where(is_diag & is_live, 0, jnp.where(is_live, -FAR, FAR))
    held_at = ((iota((total, LANES), 0) // per_group == g)
               & (iota((total, LANES), 0) % per_group == iota((total, LANES), 1)))
    back = nn(
        jnp.where(used, place, float(cap)).astype(jnp.bfloat16),
        held_at.astype(jnp.float32).astype(jnp.bfloat16),
    )
    inv_ref[...] = back.astype(jnp.int32)


def greet(g, d, n_ctx, n_head):
    barrier = pltpu.get_barrier_semaphore()

    def plane(o, _):
        pl.semaphore_signal(
            barrier, inc=1, device_id=(g, lax.rem(d + o, n_head)), device_id_type=MESH
        )
        return 0

    lax.fori_loop(1, n_head, plane, 0)

    def line(o, _):
        pl.semaphore_signal(
            barrier, inc=1, device_id=(lax.rem(g + o, n_ctx), d), device_id_type=MESH
        )
        return 0

    lax.fori_loop(1, n_ctx, line, 0)
    pl.semaphore_wait(barrier, n_head + n_ctx - 2)


def await_bytes(ref, sem):
    pltpu.make_async_copy(ref, ref, sem).wait()


def near_first(s, n):
    return lax.rem((s % 2) * ((s + 1) // 2) + (1 - s % 2) * (n - s // 2), n)


def far_first(s, n):
    return n // 2 + ((s + 1) // 2) * (1 - 2 * (s % 2))


def reach(rows, quarter, m):
    shape = (quarter, rows)
    return iota(shape, 1) // 8 - iota(shape, 0) - m * quarter


def scaled(thr, i, c, n_ctx, cap, quarter, gap, raw):
    factor = (LANES ** -0.5) * LOG2E
    parts = []
    for k in range(cap):
        part = raw[k * quarter : (k + 1) * quarter] * factor
        parts.append(jnp.where(gap >= thr[i, k * n_ctx + c], part, NEG))
    return jnp.concatenate(parts, axis=0)


def main_kernel(
    dims,
    ids,
    thr,
    inv,
    q,
    do,
    dl,
    keys,
    vals,
    gq_out,
    gk_out,
    gv_out,
    k_held,
    v_held,
    k_send,
    v_send,
    k_got,
    v_got,
    q_got,
    do_got,
    dl_got,
    weights,
    tops,
    stats,
    shared,
    lse,
    delta,
    gq_t,
    gq_send,
    gq_got,
    gk_send,
    gv_send,
    k_back,
    v_back,
    k_acc,
    v_acc,
    k_sum,
    v_sum,
    ss,
    rs,
    rs_line,
):
    n_ctx, n_head, members, per_dev, quarter, cap, own, rows = dims
    g = lax.axis_index("ctx")
    d = lax.axis_index("head")
    h = d // members
    m = d % members
    core = d % 2
    chip = d // 2
    chips = n_head // 2
    partner = 2 * chip + 1 - core
    per = rows // LANES
    scaling = LANES ** -0.5
    greet(g, d, n_ctx, n_head)

    def send(src, dst, s_sem, r_sem, to):
        pltpu.make_async_remote_copy(
            src_ref=src,
            dst_ref=dst,
            send_sem=s_sem,
            recv_sem=r_sem,
            device_id=to,
            device_id_type=MESH,
        ).start()

    def held_pair(src, p, held):
        return (
            src.at[p // members, :, 0, pl.ds((p % members) * quarter, quarter), :],
            held.at[pl.ds(per_dev * d, per_dev)],
        )

    for n, src, held in ((0, keys, k_held), (1, vals, v_held)):

        def send_kv(o, _, n=n, src=src, held=held):
            p = lax.rem(d + o, n_head)
            send(*held_pair(src, p, held), ss.at[n], rs.at[n], (g, p))
            return 0

        lax.fori_loop(1, n_head, send_kv, 0)
        pltpu.make_async_copy(*held_pair(src, d, held), rs.at[n]).start()

    def send_q(o, _):
        t = lax.rem(chip + o, chips)
        send(q.at[2 * t // members], q_got.at[d], ss.at[2], rs.at[2], (g, 2 * t))
        send(do.at[2 * t // members], do_got.at[d], ss.at[2], rs.at[3], (g, 2 * t + 1))
        return 0

    lax.fori_loop(1, chips, send_q, 0)

    @pl.when(core == 0)
    def _():
        pltpu.make_async_copy(q.at[h], q_got.at[d], rs.at[2]).start()
        send(do.at[h], do_got.at[d], ss.at[2], rs.at[3], (g, partner))

    @pl.when(core == 1)
    def _():
        pltpu.make_async_copy(do.at[h], do_got.at[d], rs.at[3]).start()
        send(q.at[h], q_got.at[d], ss.at[2], rs.at[2], (g, partner))

    def send_d(o, _):
        p = lax.rem(d + o, n_head)
        send(dl.at[p // members], dl_got.at[d], ss.at[4], rs.at[4], (g, p))
        return 0

    lax.fori_loop(1, n_head, send_d, 0)
    pltpu.make_async_copy(dl.at[h], dl_got.at[d], rs.at[4]).start()

    for n, held, packed, out in ((0, k_held, k_send, k_got), (1, v_held, v_send, v_got)):
        await_bytes(held, rs.at[n])

        def pack(s, _, n=n, held=held, packed=packed, out=out):
            off = near_first(s, n_ctx)
            c = lax.rem(g + off, n_ctx)
            for k in range(cap):
                packed[c, k] = held[ids[c, k]]

            @pl.when(s > 0)
            def _():
                send(packed.at[c], out.at[g], ss.at[5 + n], rs_line.at[n, off], (c, d))

            @pl.when(s == 0)
            def _():
                pltpu.make_async_copy(packed.at[c], out.at[g], rs_line.at[n, off]).start()

            return 0

        lax.fori_loop(0, n_ctx, pack, 0)

    @pl.when(core == 0)
    def _():
        await_bytes(q_got, rs.at[2])
        send(q_got, q_got, ss.at[3], rs.at[2], (g, partner))

    @pl.when(core == 1)
    def _():
        await_bytes(do_got, rs.at[3])
        send(do_got, do_got, ss.at[3], rs.at[3], (g, partner))
        await_bytes(q_got, rs.at[2])

    gap = reach(rows, quarter, m)
    stats[...] = jnp.where(iota(stats.shape, 0) < 4, NEG, 0.0)

    def weigh(s, _):
        off = near_first(s, n_ctx)
        c = lax.rem(g - off + n_ctx, n_ctx)
        await_bytes(k_got.at[c], rs_line.at[0, off])

        def one(i, _):
            key = k_got[c].reshape(cap * quarter, LANES)
            query = q_got[pl.ds(i * per, per)].reshape(rows, LANES)
            score = scaled(thr, i, c, n_ctx, cap, quarter, gap, nt(key, query))
            old = stats[pl.ds(i, 1)]
            new = jnp.maximum(old, jnp.max(score, axis=0, keepdims=True))
            weight = jnp.exp2(score - new)
            weights[c, i] = weight
            tops[c, pl.ds(i, 1)] = new
            stats[pl.ds(i, 1)] = new
            stats[pl.ds(4 + i, 1)] = stats[pl.ds(4 + i, 1)] * jnp.exp2(old - new) + jnp.sum(
                weight, axis=0, keepdims=True
            )
            return 0

        lax.fori_loop(0, own, one, 0)
        return 0

    lax.fori_loop(0, n_ctx, weigh, 0)

    for o in range(1, members):
        to = (g, h * members + lax.rem(m + o, members))
        send(stats, shared.at[m], ss.at[7], rs.at[5], to)
    pltpu.make_async_copy(stats, shared.at[m], rs.at[5]).start()

    @pl.when(core == 0)
    def _():
        await_bytes(do_got, rs.at[3])

    await_bytes(dl_got, rs.at[4])
    for i in range(own):
        delta[i : i + 1] = jnp.concatenate([dl_got[i * per + e] for e in range(per)], axis=1)
    gq_t[...] = jnp.zeros_like(gq_t)
    await_bytes(shared, rs.at[5])
    for i in range(own):
        each = [shared[e, i : i + 1] for e in range(members)]
        top = functools.reduce(jnp.maximum, each)
        mass = sum(shared[e, 4 + i : 5 + i] * jnp.exp2(each[e] - top) for e in range(members))
        lse[i : i + 1] = top + jnp.log2(mass)

    def grads(s, _):
        off = far_first(s, n_ctx)
        c = lax.rem(g + off, n_ctx)
        await_bytes(v_got.at[c], rs_line.at[1, lax.rem(n_ctx - off, n_ctx)])
        key = k_got[c].reshape(cap * quarter, LANES)
        value = v_got[c].reshape(cap * quarter, LANES)
        key_t = key.T

        def one(i, carry):
            acc_k, acc_v = carry
            query = q_got[pl.ds(i * per, per)].reshape(rows, LANES)
            cot = do_got[pl.ds(i * per, per)].reshape(rows, LANES)
            prob = weights[c, i] * jnp.exp2(tops[c, pl.ds(i, 1)] - lse[pl.ds(i, 1)])
            dscore = (prob * (nt(value, cot) - delta[pl.ds(i, 1)])).astype(jnp.bfloat16)
            acc_v = acc_v + nn(prob.astype(jnp.bfloat16), cot)
            acc_k = acc_k + nn(dscore, query)
            gq_t[i] += nn(key_t, dscore)
            return acc_k, acc_v

        zero = jnp.zeros((cap * quarter, LANES), jnp.float32)
        acc_k, acc_v = lax.fori_loop(0, own, one, (zero, zero))
        gk_send[c] = (acc_k * scaling).astype(gk_send.dtype).reshape(cap, quarter, LANES)
        gv_send[c] = acc_v.astype(gv_send.dtype).reshape(cap, quarter, LANES)
        for n, packed, back in ((0, gk_send, k_back), (1, gv_send, v_back)):
            for e in range(n_ctx):

                @pl.when(off == e)
                def _(n=n, packed=packed, place=back[e].at[pl.ds(0, cap)], e=e):
                    if e > 0:
                        send(packed.at[c], place, ss.at[8 + n], rs_line.at[2 + n, e], (c, d))
                    else:
                        pltpu.make_async_copy(packed.at[c], place, rs_line.at[2 + n, e]).start()

        return 0

    lax.fori_loop(0, n_ctx, grads, 0)

    def turn(i, _):
        part = (gq_t[i].T * scaling).astype(gq_send.dtype)
        gq_send[pl.ds(i * per, per)] = part.reshape(per, LANES, LANES)
        return 0

    lax.fori_loop(0, own, turn, 0)

    def send_gq(o, _):
        p = lax.rem(d + o, n_head)
        send(gq_send.at[p], gq_got.at[d], ss.at[10], rs.at[6], (g, p))
        return 0

    lax.fori_loop(1, n_head, send_gq, 0)
    pltpu.make_async_copy(gq_send.at[d], gq_got.at[d], rs.at[6]).start()

    for c in range(n_ctx):
        k_back[c][cap] = jnp.zeros(k_back[c].shape[1:], k_back[c].dtype)
        v_back[c][cap] = jnp.zeros(v_back[c].shape[1:], v_back[c].dtype)

    def picked(back, offs, l):
        acc = None
        for off in offs:
            c = lax.rem(g - off + n_ctx, n_ctx)
            term = back[off][inv[c, l]].astype(jnp.float32)
            acc = term if acc is None else acc + term
        return acc

    half = n_ctx // 2
    pairs = [(0, half)] + [(half - e, half + e) for e in range(1, half)]
    for step, offs in enumerate(pairs):
        for off in offs:
            c = lax.rem(g - off + n_ctx, n_ctx)
            await_bytes(gk_send.at[c], rs_line.at[2, off])
            await_bytes(gv_send.at[c], rs_line.at[3, off])
        if step < len(pairs) - 1:

            def add_up(l, _, offs=offs, step=step):
                for back, acc in ((k_back, k_acc), (v_back, v_acc)):
                    term = picked(back, offs, l)
                    acc[l] = term if step == 0 else acc[l] + term
                return 0

            lax.fori_loop(0, per_dev * n_head, add_up, 0)
        else:

            def finish(o, _, offs=offs):
                p = lax.rem(d + o, n_head)
                for n, back, acc, total, out in (
                    (0, k_back, k_acc, k_sum, gk_out),
                    (1, v_back, v_acc, v_sum, gv_out),
                ):
                    for e in range(per_dev):
                        l = per_dev * p + e
                        total[l] = (acc[l] + picked(back, offs, l)).astype(total.dtype)
                    src = total.at[pl.ds(per_dev * p, per_dev)]
                    place = out.at[h, :, 0, pl.ds(m * quarter, quarter), :]

                    @pl.when(o < n_head)
                    def _(n=n, src=src, place=place):
                        send(src, place, ss.at[11 + n], rs.at[7 + n], (g, p))

                    @pl.when(o == n_head)
                    def _(n=n, src=src, place=place):
                        pltpu.make_async_copy(src, place, rs.at[7 + n]).start()

                return 0

            lax.fori_loop(1, n_head + 1, finish, 0)

    await_bytes(gq_got, rs.at[6])

    def add_q(e, _):
        acc = gq_got[members * e].astype(jnp.float32)
        for o in range(1, members):
            acc = acc + gq_got[members * e + o].astype(jnp.float32)
        gq_out[e] = acc.astype(gq_out.dtype)
        return 0

    lax.fori_loop(0, n_head // members, add_q, 0)
    await_bytes(k_sum, rs.at[7])
    await_bytes(v_sum, rs.at[8])
    for n, ref in ((0, k_held), (1, v_held), (11, k_sum), (12, v_sum)):
        await_bytes(ref.at[pl.ds(0, per_dev * (n_head - 1))], ss.at[n])
    for n, ref in ((2, q_got), (4, dl_got), (10, gq_send)):
        await_bytes(ref.at[pl.ds(0, n_head - 1)], ss.at[n])
    await_bytes(q_got, ss.at[3])
    for n, ref in ((5, k_send), (6, v_send), (8, gk_send), (9, gv_send)):
        await_bytes(ref.at[pl.ds(0, n_ctx - 1)], ss.at[n])
    await_bytes(shared.at[pl.ds(0, members - 1)], ss.at[7])


def body(queries, keys, values, outputs, grad_out, block_ids, block_counts):
    f32, bf16, i32 = jnp.float32, jnp.bfloat16, jnp.int32
    n_ctx = lax.axis_size("ctx")
    n_head = lax.axis_size("head")
    kv, per_dev, _, blk, dh = keys.shape
    tokens, heads, _ = queries.shape
    members = n_head // kv
    quarter = blk // members
    group = heads // kv
    per_group = per_dev * n_head
    blocks, _, slots = block_ids.shape
    own = blocks // n_ctx
    cap = (slots + own + n_ctx - 2) // n_ctx
    part = tokens * group
    rows = blk * group
    any_ = whole(pl.ANY)
    vm = whole(VMEM)
    sm = whole(SMEM)
    limit = 60 * 2**20

    def by_kv(x):
        return jnp.transpose(x.reshape(tokens, kv, group, dh), (1, 0, 2, 3)).reshape(kv, part, dh)

    delta = jnp.sum(grad_out.astype(f32) * outputs.astype(f32), axis=2)
    delta = jnp.transpose(delta.reshape(tokens, kv, group), (1, 0, 2)).reshape(kv, 1, part)
    q8 = by_kv(queries)
    do8 = by_kv(grad_out)

    ids, thr, inv = pl.pallas_call(
        functools.partial(plan_kernel, (n_ctx, members, per_group, own, cap)),
        out_shape=[jax.ShapeDtypeStruct((8, LANES), i32)] * 3,
        in_specs=[vm, vm],
        out_specs=[vm] * 3,
        compiler_params=pltpu.CompilerParams(vmem_limit_bytes=limit),
        name="plan",
    )(block_ids, block_counts)

    packed = (n_ctx, cap, quarter, dh)
    back = [VMEM((cap + 1, quarter, dh), bf16)] * n_ctx
    held = (per_group, quarter, dh)
    spread = (n_head, part, dh)
    gq8, grad_keys, grad_values = pl.pallas_call(
        functools.partial(
            main_kernel, (n_ctx, n_head, members, per_dev, quarter, cap, own, rows)
        ),
        out_shape=[
            jax.ShapeDtypeStruct((kv, part, dh), bf16),
            jax.ShapeDtypeStruct(keys.shape, bf16),
            jax.ShapeDtypeStruct(keys.shape, bf16),
        ],
        in_specs=[sm] * 3 + [any_] * 5,
        out_specs=[vm, any_, any_],
        scratch_shapes=[
            VMEM(held, bf16),
            VMEM(held, bf16),
            VMEM(packed, bf16),
            VMEM(packed, bf16),
            VMEM(packed, bf16),
            VMEM(packed, bf16),
            VMEM(spread, bf16),
            VMEM(spread, bf16),
            VMEM((n_head, 1, part), f32),
            VMEM((n_ctx, own, cap * quarter, rows), f32),
            VMEM((n_ctx, own, rows), f32),
            VMEM((8, rows), f32),
            VMEM((members, 8, rows), f32),
            VMEM((own, rows), f32),
            VMEM((own, rows), f32),
            VMEM((own, dh, rows), f32),
            VMEM(spread, bf16),
            VMEM(spread, bf16),
            VMEM(packed, bf16),
            VMEM(packed, bf16),
            back,
            back,
            VMEM(held, f32),
            VMEM(held, f32),
            VMEM(held, bf16),
            VMEM(held, bf16),
            pltpu.SemaphoreType.DMA((13,)),
            pltpu.SemaphoreType.DMA((9,)),
            pltpu.SemaphoreType.DMA((4, n_ctx)),
        ],
        compiler_params=pltpu.CompilerParams(
            collective_id=0, has_side_effects=True, vmem_limit_bytes=limit
        ),
        name="main",
    )(ids, thr, inv, q8, do8, delta, keys, values)
    grad_queries = jnp.transpose(gq8.reshape(kv, tokens, group, dh), (1, 0, 2, 3)).reshape(
        tokens, heads, dh
    )
    return grad_queries, grad_keys, grad_values


def solution(mesh):
    tok = P(("ctx", "head"), None, None)
    cached = P(None, "head", "ctx", None, None)
    return jax.shard_map(
        body,
        mesh=mesh,
        in_specs=(tok, cached, cached, tok, tok, P(), P()),
        out_specs=(tok, cached, cached),
        check_vma=False,
    )
```

```python
import functools

import jax
import jax.numpy as jnp
from jax import lax
from jax.experimental import pallas as pl
from jax.experimental.pallas import tpu as pltpu
from jax.sharding import PartitionSpec as P

MESH = pl.DeviceIdType.MESH
VMEM = pltpu.VMEM
SMEM = pltpu.SMEM
NEG = -1e30
LOG2E = 1.4426950408889634
LANES = 128
FAR = 4096
HOOK = 2
HOOK_SUM = 6


def whole(space):
    return pl.BlockSpec(memory_space=space)


def nt(a, b):
    return lax.dot_general(a, b, (((1,), (1,)), ((), ())), preferred_element_type=jnp.float32)


def nn(a, b):
    return lax.dot_general(a, b, (((1,), (0,)), ((), ())), preferred_element_type=jnp.float32)


def iota(shape, dim):
    return lax.broadcasted_iota(jnp.int32, shape, dim)


def plan(dims, lists_ref, counts_ref, ids_ref, thr_ref, inv_ref):
    n_ctx, members, per_group, own, cap = dims
    g = lax.axis_index("ctx")
    h = lax.axis_index("head") // members
    blocks, kv, slots = lists_ref.shape
    total = n_ctx * per_group
    pick = iota((blocks, kv, slots), 1) == h
    lists = jnp.sum(jnp.where(pick, lists_ref[...].astype(jnp.float32), 0.0), axis=1)
    count = jnp.sum(
        jnp.where(iota((kv, blocks), 0) == h, counts_ref[...].astype(jnp.float32), 0.0),
        axis=0,
        keepdims=True,
    )
    square = iota((blocks, blocks), 0) == iota((blocks, blocks), 1)
    count = jnp.sum(jnp.where(square, count, 0.0), axis=1, keepdims=True)
    lists = jnp.where(iota((blocks, slots), 1).astype(jnp.float32) < count, lists, -1.0)
    col = iota((1, total), 1)
    col_id = ((col % per_group) * n_ctx + col // per_group).astype(jnp.float32)
    live = jnp.zeros((blocks, total), jnp.float32)
    for n in range(slots):
        live = jnp.where(lists[:, n : n + 1] == col_id, 1.0, live)
    low = live.astype(jnp.bfloat16)
    of_group = (iota((8, blocks), 1) // own == iota((8, blocks), 0)).astype(jnp.float32)
    used = nn(of_group.astype(jnp.bfloat16), low) > 0.5
    used_f = used.astype(jnp.float32)
    before = (iota((total, total), 0) // per_group == iota((total, total), 1) // per_group) & (
        iota((total, total), 0) < iota((total, total), 1)
    )
    place = nn(used_f.astype(jnp.bfloat16), before.astype(jnp.float32).astype(jnp.bfloat16))
    rows8 = iota((8, blocks), 0)
    own_rows = ((iota((8, blocks), 1) == own * g + rows8) & (rows8 < own)).astype(jnp.float32)
    own_live = nn(own_rows.astype(jnp.bfloat16), low)
    row8 = iota((8, total), 0)
    diag = (
        (col_id == (total - blocks + own * g + row8).astype(jnp.float32)) & (row8 < own)
    ).astype(jnp.float32)
    key_row = iota((total, 2 * LANES), 0)
    lane = iota((total, 2 * LANES), 1)
    key_group = key_row // per_group
    key_local = key_row % per_group
    got = jnp.zeros((24, 2 * LANES), jnp.float32)
    for k in range(cap):
        match = jnp.where(used & (place == k), 1.0, 0.0)
        mine = jnp.sum(jnp.where(row8 == g, match, 0.0), axis=0, keepdims=True)
        left = jnp.concatenate([match, own_live * mine, diag * mine], axis=0)
        right = jnp.where(
            lane == k,
            jnp.where(key_group == g, key_local, 0),
            jnp.where(lane == LANES + k * n_ctx + key_group, 1, 0),
        )
        got = got + nn(left.astype(jnp.bfloat16), right.astype(jnp.float32).astype(jnp.bfloat16))
    ids_ref[...] = got[0:8, :LANES].astype(jnp.int32)
    is_live = got[8:16, LANES:] > 0.5
    is_diag = got[16:24, LANES:] > 0.5
    thr_ref[...] = jnp.where(is_diag & is_live, 0, jnp.where(is_live, -FAR, FAR))
    held_at = ((iota((total, LANES), 0) // per_group == g)
               & (iota((total, LANES), 0) % per_group == iota((total, LANES), 1)))
    back = nn(
        jnp.where(used, place, float(cap)).astype(jnp.bfloat16),
        held_at.astype(jnp.float32).astype(jnp.bfloat16),
    )
    inv_ref[...] = back.astype(jnp.int32)


def greet(g, d, n_ctx, n_head):
    barrier = pltpu.get_barrier_semaphore()

    def plane(o, _):
        pl.semaphore_signal(
            barrier, inc=1, device_id=(g, lax.rem(d + o, n_head)), device_id_type=MESH
        )
        return 0

    lax.fori_loop(1, n_head, plane, 0)

    def line(o, _):
        pl.semaphore_signal(
            barrier, inc=1, device_id=(lax.rem(g + o, n_ctx), d), device_id_type=MESH
        )
        return 0

    lax.fori_loop(1, n_ctx, line, 0)
    pl.semaphore_wait(barrier, n_head + n_ctx - 2)


def await_bytes(ref, sem):
    pltpu.make_async_copy(ref, ref, sem).wait()


def near_first(s, n):
    return lax.rem((s % 2) * ((s + 1) // 2) + (1 - s % 2) * (n - s // 2), n)


def far_first(s, n):
    return n // 2 + ((s + 1) // 2) * (1 - 2 * (s % 2))


def reach(rows, quarter, m):
    shape = (quarter, rows)
    return iota(shape, 1) // 8 - iota(shape, 0) - m * quarter


def scaled(thr, i, c, n_ctx, cap, quarter, gap, raw):
    factor = (LANES ** -0.5) * LOG2E
    parts = []
    for k in range(cap):
        part = raw[k * quarter : (k + 1) * quarter] * factor
        parts.append(jnp.where(gap >= thr[i, k * n_ctx + c], part, NEG))
    return jnp.concatenate(parts, axis=0)


def main_kernel(
    dims,
    lists,
    counts,
    q,
    do,
    out8,
    keys,
    vals,
    gq_out,
    gk_out,
    gv_out,
    plans,
    ids,
    thr,
    inv,
    dl_send,
    k_held,
    v_held,
    k_send,
    v_send,
    k_got,
    v_got,
    q_got,
    do_got,
    dl_got,
    weights,
    tops,
    stats,
    shared,
    lse,
    delta,
    gq_t,
    gq_send,
    gq_pair,
    gq_got,
    gk_send,
    gv_send,
    k_back,
    v_back,
    k_sum,
    v_sum,
    ss,
    rs,
    rs_line,
    local_sem,
):
    n_ctx, n_head, members, per_dev, quarter, cap, own, rows = dims
    g = lax.axis_index("ctx")
    d = lax.axis_index("head")
    h = d // members
    m = d % members
    core = d % 2
    chip = d // 2
    chips = n_head // 2
    partner = 2 * chip + 1 - core
    per = rows // LANES
    half = n_head // 2
    scaling = LANES ** -0.5
    greet(g, d, n_ctx, n_head)

    def send(src, dst, s_sem, r_sem, to):
        pltpu.make_async_remote_copy(
            src_ref=src,
            dst_ref=dst,
            send_sem=s_sem,
            recv_sem=r_sem,
            device_id=to,
            device_id_type=MESH,
        ).start()

    def held_pair(src, p, held):
        return (
            src.at[p // members, :, 0, pl.ds((p % members) * quarter, quarter), :],
            held.at[pl.ds(per_dev * d, per_dev)],
        )

    def send_held(n, src, held):
        def one(o, _):
            p = lax.rem(d + o, n_head)
            send(*held_pair(src, p, held), ss.at[n], rs.at[n], (g, p))
            return 0

        lax.fori_loop(1, n_head, one, 0)
        pltpu.make_async_copy(*held_pair(src, d, held), rs.at[n]).start()

    def held_left(n, held):
        await_bytes(held.at[pl.ds(0, per_dev * (n_head - 1))], ss.at[n])

    def send_rows(src, got, n, to_core):
        def one(o, _):
            t = lax.rem(chip + o, chips)
            send(src.at[2 * t // members], got.at[d], ss.at[n], rs.at[n], (g, 2 * t + to_core))
            return 0

        lax.fori_loop(1, chips, one, 0)

        @pl.when(core == to_core)
        def _():
            pltpu.make_async_copy(src.at[h], got.at[d], rs.at[n]).start()

        @pl.when(core != to_core)
        def _():
            send(src.at[h], got.at[d], ss.at[n], rs.at[n], (g, partner))

    def rows_left(got, n, to_core):
        await_bytes(got.at[pl.ds(0, chips - 1)], ss.at[n])

        @pl.when(core != to_core)
        def _():
            await_bytes(got.at[0], ss.at[n])

    def forward(got, n, to_core):
        @pl.when(core == to_core)
        def _():
            await_bytes(got, rs.at[n])
            send(got, got, ss.at[4], rs.at[n], (g, partner))

    def send_retained(n, held, packed, got):
        await_bytes(held, rs.at[n])

        def one(s, _):
            off = near_first(s, n_ctx)
            c = lax.rem(g + off, n_ctx)
            for k in range(cap):
                packed[c, k] = held[jnp.clip(ids[c, k], 0, per_dev * n_head - 1)]

            @pl.when(s > 0)
            def _():
                send(packed.at[c], got.at[g], ss.at[6 + n], rs_line.at[n, off], (c, d))

            @pl.when(s == 0)
            def _():
                pltpu.make_async_copy(packed.at[c], got.at[g], rs_line.at[n, off]).start()

            return 0

        lax.fori_loop(0, n_ctx, one, 0)

    send_held(0, keys, k_held)

    plan((n_ctx, members, per_dev * n_head, own, cap), lists, counts, *[plans.at[e] for e in range(3)])
    for e, place in enumerate((ids, thr, inv)):
        pltpu.make_async_copy(plans.at[e], place, local_sem.at[e]).start()
    for e in range(n_head // members):
        product = do[e].astype(jnp.float32) * out8[e].astype(jnp.float32)
        dl_send[e] = jnp.sum(product.T, axis=0, keepdims=True)
    for e, place in enumerate((ids, thr, inv)):
        pltpu.make_async_copy(plans.at[e], place, local_sem.at[e]).wait()

    held_left(0, k_held)
    send_rows(q, q_got, 2, 0)
    send_retained(0, k_held, k_send, k_got)
    rows_left(q_got, 2, 0)
    send_held(1, vals, v_held)
    forward(q_got, 2, 0)

    @pl.when(core == 1)
    def _():
        await_bytes(q_got, rs.at[2])

    def more():
        held_left(1, v_held)
        send_rows(do, do_got, 3, 1)

        def send_delta(o, _):
            p = lax.rem(d + o, n_head)
            send(dl_send.at[p // members], dl_got.at[d], ss.at[5], rs.at[4], (g, p))
            return 0

        lax.fori_loop(1, n_head, send_delta, 0)
        pltpu.make_async_copy(dl_send.at[h], dl_got.at[d], rs.at[4]).start()
        send_retained(1, v_held, v_send, v_got)

    gap = reach(rows, quarter, m)
    stats[...] = jnp.where(iota(stats.shape, 0) < 4, NEG, 0.0)

    def weigh(s, _):
        off = near_first(s, n_ctx)
        c = lax.rem(g - off + n_ctx, n_ctx)
        await_bytes(k_got.at[c], rs_line.at[0, off])

        @pl.when(s == HOOK)
        def _():
            more()

        for i in range(own):
            key = k_got[c].reshape(cap * quarter, LANES)
            query = q_got[pl.ds(i * per, per)].reshape(rows, LANES)
            score = scaled(thr, i, c, n_ctx, cap, quarter, gap, nt(key, query))
            old = stats[pl.ds(i, 1)]
            new = jnp.maximum(old, jnp.max(score, axis=0, keepdims=True))
            weight = jnp.exp2(score - new)
            weights[c, i] = weight
            tops[c, pl.ds(i, 1)] = new
            stats[pl.ds(i, 1)] = new
            stats[pl.ds(4 + i, 1)] = stats[pl.ds(4 + i, 1)] * jnp.exp2(old - new) + jnp.sum(
                weight, axis=0, keepdims=True
            )
        return 0

    lax.fori_loop(0, n_ctx, weigh, 0)

    for o in range(1, members):
        to = (g, h * members + lax.rem(m + o, members))
        send(stats, shared.at[m], ss.at[8], rs.at[5], to)
    pltpu.make_async_copy(stats, shared.at[m], rs.at[5]).start()
    gq_t[...] = jnp.zeros_like(gq_t)
    await_bytes(dl_got, rs.at[4])
    for i in range(own):
        delta[i : i + 1] = jnp.concatenate([dl_got[i * per + e] for e in range(per)], axis=1)
    forward(do_got, 3, 1)
    await_bytes(shared, rs.at[5])
    for i in range(own):
        each = [shared[e, i : i + 1] for e in range(members)]
        top = functools.reduce(jnp.maximum, each)
        mass = sum(shared[e, 4 + i : 5 + i] * jnp.exp2(each[e] - top) for e in range(members))
        lse[i : i + 1] = top + jnp.log2(mass)

    @pl.when(core == 0)
    def _():
        await_bytes(do_got, rs.at[3])

    def probs(c, i):
        return weights[c, i] * jnp.exp2(tops[c, pl.ds(i, 1)] - lse[pl.ds(i, 1)])

    def send_back(n, s, off, c, packed, back):
        place = back.at[g, pl.ds(0, cap)]

        @pl.when(s < n_ctx - 1)
        def _():
            send(packed.at[c], place, ss.at[9 + n], rs_line.at[2 + n, off], (c, d))

        @pl.when(s == n_ctx - 1)
        def _():
            pltpu.make_async_copy(packed.at[c], place, rs_line.at[2 + n, off]).start()

    zero = jnp.zeros((cap * quarter, LANES), jnp.float32)
    shape = (cap, quarter, LANES)

    def value_grads(s, _):
        off = far_first(s, n_ctx)
        c = lax.rem(g + off, n_ctx)

        acc = zero
        for i in range(own):
            cot = do_got[pl.ds(i * per, per)].reshape(rows, LANES)
            acc = acc + nn(probs(c, i).astype(jnp.bfloat16), cot)
        gv_send[c] = acc.astype(gv_send.dtype).reshape(shape)
        send_back(1, s, off, c, gv_send, v_back)
        return 0

    lax.fori_loop(0, n_ctx, value_grads, 0)

    for c in range(n_ctx):
        k_back[c, cap] = jnp.zeros(k_back.shape[2:], k_back.dtype)
        v_back[c, cap] = jnp.zeros(v_back.shape[2:], v_back.dtype)

    def finish(n, packed, back, total, out):
        for off in range(n_ctx):
            await_bytes(packed.at[0], rs_line.at[2 + n, off])

        def one(o, _):
            p = lax.rem(d + o, n_head)
            for e in range(per_dev):
                l = per_dev * p + e
                acc = back[0, jnp.clip(inv[0, l], 0, cap)].astype(jnp.float32)
                for c in range(1, n_ctx):
                    acc = acc + back[c, jnp.clip(inv[c, l], 0, cap)].astype(jnp.float32)
                total[l] = acc.astype(total.dtype)
            src = total.at[pl.ds(per_dev * p, per_dev)]
            place = out.at[h, :, 0, pl.ds(m * quarter, quarter), :]

            @pl.when(o < n_head)
            def _():
                send(src, place, ss.at[12 + n], rs.at[8 + n], (g, p))

            @pl.when(o == n_head)
            def _():
                pltpu.make_async_copy(src, place, rs.at[8 + n]).start()

            return 0

        lax.fori_loop(1, n_head + 1, one, 0)

    def key_grads(s, _):
        off = far_first(s, n_ctx)
        c = lax.rem(g + off, n_ctx)
        await_bytes(v_got.at[c], rs_line.at[1, lax.rem(n_ctx - off, n_ctx)])
        key_t = k_got[c].reshape(cap * quarter, LANES).T
        value = v_got[c].reshape(cap * quarter, LANES)

        @pl.when(s == HOOK_SUM)
        def _():
            finish(1, gv_send, v_back, v_sum, gv_out)

        acc = zero
        for i in range(own):
            query = q_got[pl.ds(i * per, per)].reshape(rows, LANES)
            cot = do_got[pl.ds(i * per, per)].reshape(rows, LANES)
            dscore = (probs(c, i) * (nt(value, cot) - delta[pl.ds(i, 1)])).astype(jnp.bfloat16)
            gq_t[i] += nn(key_t, dscore)
            acc = acc + nn(dscore, query)
        gk_send[c] = (acc * scaling).astype(gk_send.dtype).reshape(shape)
        send_back(0, s, off, c, gk_send, k_back)
        return 0

    lax.fori_loop(0, n_ctx, key_grads, 0)

    def theirs(e, _):
        i = (own // 2) * (1 - core) + e
        part = (gq_t[i].T * scaling).astype(gq_send.dtype)
        gq_send[pl.ds(i * per, per)] = part.reshape(per, LANES, LANES)
        return 0

    lax.fori_loop(0, own // 2, theirs, 0)
    send(
        gq_send.at[pl.ds(half * (1 - core), half)], gq_pair, ss.at[11], rs.at[6], (g, partner)
    )

    await_bytes(gq_pair, rs.at[6])

    def ours(e, _):
        i = (own // 2) * core + e
        part = (gq_t[i].T * scaling).reshape(per, LANES, LANES)
        part = part + gq_pair[pl.ds(e * per, per)].astype(jnp.float32)
        gq_send[pl.ds(i * per, per)] = part.astype(gq_send.dtype)
        return 0

    lax.fori_loop(0, own // 2, ours, 0)

    def send_gq(o, _):
        p = half * core + lax.rem(d + o, half)

        @pl.when(p != d)
        def _():
            send(gq_send.at[p], gq_got.at[chip], ss.at[14], rs.at[7], (g, p))

        @pl.when(p == d)
        def _():
            pltpu.make_async_copy(gq_send.at[p], gq_got.at[chip], rs.at[7]).start()

        return 0

    lax.fori_loop(0, half, send_gq, 0)

    finish(0, gk_send, k_back, k_sum, gk_out)

    await_bytes(gq_got, rs.at[7])
    pair = members // 2

    def add_q(e, _):
        acc = gq_got[pair * e].astype(jnp.float32)
        for o in range(1, pair):
            acc = acc + gq_got[pair * e + o].astype(jnp.float32)
        gq_out[e] = acc.astype(gq_out.dtype)
        return 0

    lax.fori_loop(0, n_head // members, add_q, 0)
    await_bytes(k_sum, rs.at[8])
    await_bytes(v_sum, rs.at[9])
    rows_left(do_got, 3, 1)
    await_bytes(q_got, ss.at[4])
    await_bytes(dl_got.at[pl.ds(0, n_head - 1)], ss.at[5])
    for n, ref in ((6, k_send), (7, v_send), (9, gk_send), (10, gv_send)):
        await_bytes(ref.at[pl.ds(0, n_ctx - 1)], ss.at[n])
    await_bytes(shared.at[pl.ds(0, members - 1)], ss.at[8])
    await_bytes(gq_pair, ss.at[11])
    for n, ref in ((12, k_sum), (13, v_sum)):
        await_bytes(ref.at[pl.ds(0, per_dev * (n_head - 1))], ss.at[n])
    await_bytes(gq_send.at[pl.ds(0, half - 1)], ss.at[14])

    @pl.when(d // half != core)
    def _():
        await_bytes(gq_send.at[0], ss.at[14])


def body(queries, keys, values, outputs, grad_out, block_ids, block_counts):
    f32, bf16, i32 = jnp.float32, jnp.bfloat16, jnp.int32
    n_ctx = lax.axis_size("ctx")
    n_head = lax.axis_size("head")
    kv, per_dev, _, blk, dh = keys.shape
    tokens, heads, _ = queries.shape
    members = n_head // kv
    quarter = blk // members
    group = heads // kv
    per_group = per_dev * n_head
    blocks, _, slots = block_ids.shape
    own = blocks // n_ctx
    cap = (slots + own + n_ctx - 2) // n_ctx
    part = tokens * group
    rows = blk * group
    any_ = whole(pl.ANY)
    vm = whole(VMEM)
    sm = whole(SMEM)
    limit = 60 * 2**20

    def by_kv(x):
        return jnp.transpose(x.reshape(tokens, kv, group, dh), (1, 0, 2, 3)).reshape(kv, part, dh)

    q8 = by_kv(queries)
    do8 = by_kv(grad_out)

    o8 = by_kv(outputs)
    packed = (n_ctx, cap, quarter, dh)
    back = (n_ctx, cap + 1, quarter, dh)
    held = (per_group, quarter, dh)
    spread = (n_head, part, dh)
    halves = (n_head // 2, part, dh)
    gq8, grad_keys, grad_values = pl.pallas_call(
        functools.partial(
            main_kernel, (n_ctx, n_head, members, per_dev, quarter, cap, own, rows)
        ),
        out_shape=[
            jax.ShapeDtypeStruct((kv, part, dh), bf16),
            jax.ShapeDtypeStruct(keys.shape, bf16),
            jax.ShapeDtypeStruct(keys.shape, bf16),
        ],
        in_specs=[vm] * 5 + [any_] * 2,
        out_specs=[vm, any_, any_],
        scratch_shapes=[
            VMEM((3, 8, LANES), i32),
            SMEM((8, LANES), i32),
            SMEM((8, LANES), i32),
            SMEM((8, LANES), i32),
            VMEM((kv, 1, part), f32),
            VMEM(held, bf16),
            VMEM(held, bf16),
            VMEM(packed, bf16),
            VMEM(packed, bf16),
            VMEM(packed, bf16),
            VMEM(packed, bf16),
            VMEM(spread, bf16),
            VMEM(spread, bf16),
            VMEM((n_head, 1, part), f32),
            VMEM((n_ctx, own, cap * quarter, rows), f32),
            VMEM((n_ctx, own, rows), f32),
            VMEM((8, rows), f32),
            VMEM((members, 8, rows), f32),
            VMEM((own, rows), f32),
            VMEM((own, rows), f32),
            VMEM((own, dh, rows), f32),
            VMEM(spread, bf16),
            VMEM(halves, bf16),
            VMEM(halves, bf16),
            VMEM(packed, bf16),
            VMEM(packed, bf16),
            VMEM(back, bf16),
            VMEM(back, bf16),
            VMEM(held, bf16),
            VMEM(held, bf16),
            pltpu.SemaphoreType.DMA((15,)),
            pltpu.SemaphoreType.DMA((10,)),
            pltpu.SemaphoreType.DMA((4, n_ctx)),
            pltpu.SemaphoreType.DMA((3,)),
        ],
        compiler_params=pltpu.CompilerParams(
            collective_id=0, has_side_effects=True, vmem_limit_bytes=limit
        ),
        name="main",
    )(block_ids, block_counts.T, q8, do8, o8, keys, values)
    grad_queries = jnp.transpose(gq8.reshape(kv, tokens, group, dh), (1, 0, 2, 3)).reshape(
        tokens, heads, dh
    )
    return grad_queries, grad_keys, grad_values


def solution(mesh):
    tok = P(("ctx", "head"), None, None)
    cached = P(None, "head", "ctx", None, None)
    return jax.shard_map(
        body,
        mesh=mesh,
        in_specs=(tok, cached, cached, tok, tok, P(), P()),
        out_specs=(tok, cached, cached),
        check_vma=False,
    )
```

```python
import functools

import jax
import jax.numpy as jnp
from jax import lax
from jax.experimental import pallas as pl
from jax.experimental.pallas import tpu as pltpu
from jax.sharding import PartitionSpec as P

MESH = pl.DeviceIdType.MESH
VMEM = pltpu.VMEM
SMEM = pltpu.SMEM
NEG = -1e30
LOG2E = 1.4426950408889634
LANES = 128
FAR = 4096
HOOK = 4
HOOK_SUM = 3
HOOK_GQ = 1


def whole(space):
    return pl.BlockSpec(memory_space=space)


def nt(a, b):
    return lax.dot_general(a, b, (((1,), (1,)), ((), ())), preferred_element_type=jnp.float32)


def nn(a, b):
    return lax.dot_general(a, b, (((1,), (0,)), ((), ())), preferred_element_type=jnp.float32)


def iota(shape, dim):
    return lax.broadcasted_iota(jnp.int32, shape, dim)


def plan(dims, lists_ref, counts_ref, ids_ref, thr_ref, inv_ref):
    n_ctx, members, per_group, own, cap = dims
    g = lax.axis_index("ctx")
    h = lax.axis_index("head") // members
    blocks, kv, slots = lists_ref.shape
    total = n_ctx * per_group
    pick = iota((blocks, kv, slots), 1) == h
    lists = jnp.sum(jnp.where(pick, lists_ref[...].astype(jnp.float32), 0.0), axis=1)
    count = jnp.sum(
        jnp.where(iota((kv, blocks), 0) == h, counts_ref[...].astype(jnp.float32), 0.0),
        axis=0,
        keepdims=True,
    )
    square = iota((blocks, blocks), 0) == iota((blocks, blocks), 1)
    count = jnp.sum(jnp.where(square, count, 0.0), axis=1, keepdims=True)
    lists = jnp.where(iota((blocks, slots), 1).astype(jnp.float32) < count, lists, -1.0)
    col = iota((1, total), 1)
    col_id = ((col % per_group) * n_ctx + col // per_group).astype(jnp.float32)
    live = jnp.zeros((blocks, total), jnp.float32)
    for n in range(slots):
        live = jnp.where(lists[:, n : n + 1] == col_id, 1.0, live)
    low = live.astype(jnp.bfloat16)
    of_group = (iota((8, blocks), 1) // own == iota((8, blocks), 0)).astype(jnp.float32)
    used = nn(of_group.astype(jnp.bfloat16), low) > 0.5
    used_f = used.astype(jnp.float32)
    before = (iota((total, total), 0) // per_group == iota((total, total), 1) // per_group) & (
        iota((total, total), 0) < iota((total, total), 1)
    )
    place = nn(used_f.astype(jnp.bfloat16), before.astype(jnp.float32).astype(jnp.bfloat16))
    rows8 = iota((8, blocks), 0)
    own_rows = ((iota((8, blocks), 1) == own * g + rows8) & (rows8 < own)).astype(jnp.float32)
    own_live = nn(own_rows.astype(jnp.bfloat16), low)
    row8 = iota((8, total), 0)
    diag = (
        (col_id == (total - blocks + own * g + row8).astype(jnp.float32)) & (row8 < own)
    ).astype(jnp.float32)
    key_row = iota((total, 2 * LANES), 0)
    lane = iota((total, 2 * LANES), 1)
    key_group = key_row // per_group
    key_local = key_row % per_group
    got = jnp.zeros((24, 2 * LANES), jnp.float32)
    for k in range(cap):
        match = jnp.where(used & (place == k), 1.0, 0.0)
        mine = jnp.sum(jnp.where(row8 == g, match, 0.0), axis=0, keepdims=True)
        left = jnp.concatenate([match, own_live * mine, diag * mine], axis=0)
        right = jnp.where(
            lane == k,
            jnp.where(key_group == g, key_local, 0),
            jnp.where(lane == LANES + k * n_ctx + key_group, 1, 0),
        )
        got = got + nn(left.astype(jnp.bfloat16), right.astype(jnp.float32).astype(jnp.bfloat16))
    ids_ref[...] = got[0:8, :LANES].astype(jnp.int32)
    is_live = got[8:16, LANES:] > 0.5
    is_diag = got[16:24, LANES:] > 0.5
    thr_ref[...] = jnp.where(is_diag & is_live, 0, jnp.where(is_live, -FAR, FAR))
    held_at = ((iota((total, LANES), 0) // per_group == g)
               & (iota((total, LANES), 0) % per_group == iota((total, LANES), 1)))
    back = nn(
        jnp.where(used, place, float(cap)).astype(jnp.bfloat16),
        held_at.astype(jnp.float32).astype(jnp.bfloat16),
    )
    inv_ref[...] = back.astype(jnp.int32)


def greet(g, d, n_ctx, n_head):
    barrier = pltpu.get_barrier_semaphore()

    def plane(o, _):
        pl.semaphore_signal(
            barrier, inc=1, device_id=(g, lax.rem(d + o, n_head)), device_id_type=MESH
        )
        return 0

    lax.fori_loop(1, n_head, plane, 0)

    def line(o, _):
        pl.semaphore_signal(
            barrier, inc=1, device_id=(lax.rem(g + o, n_ctx), d), device_id_type=MESH
        )
        return 0

    lax.fori_loop(1, n_ctx, line, 0)
    pl.semaphore_wait(barrier, n_head + n_ctx - 2)


def await_bytes(ref, sem):
    pltpu.make_async_copy(ref, ref, sem).wait()


def near_first(s, n):
    return lax.rem((s % 2) * ((s + 1) // 2) + (1 - s % 2) * (n - s // 2), n)


def far_first(s, n):
    return n // 2 + ((s + 1) // 2) * (1 - 2 * (s % 2))


def reach(rows, quarter, m):
    shape = (quarter, rows)
    return iota(shape, 1) // 8 - iota(shape, 0) - m * quarter


def scaled(thr, i, c, n_ctx, cap, quarter, gap, raw):
    factor = (LANES ** -0.5) * LOG2E
    parts = []
    for k in range(cap):
        part = raw[k * quarter : (k + 1) * quarter] * factor
        parts.append(jnp.where(gap >= thr[i, k * n_ctx + c], part, NEG))
    return jnp.concatenate(parts, axis=0)


def main_kernel(
    dims,
    lists,
    counts,
    q,
    do,
    out8,
    keys,
    vals,
    gq_out,
    gk_out,
    gv_out,
    plans,
    ids,
    thr,
    inv,
    dl_send,
    k_held,
    v_held,
    k_send,
    v_send,
    k_got,
    v_got,
    q_got,
    do_got,
    dl_got,
    weights,
    tops,
    stats,
    shared,
    lse,
    delta,
    keys_t,
    ds_held,
    gq_send,
    gq_full,
    gk_acc,
    gq_pair,
    gq_got,
    gk_send,
    gv_send,
    k_back,
    v_back,
    k_sum,
    v_sum,
    ss,
    rs,
    rs_line,
    rs_q,
    local_sem,
):
    n_ctx, n_head, members, per_dev, quarter, cap, own, rows = dims
    g = lax.axis_index("ctx")
    d = lax.axis_index("head")
    h = d // members
    m = d % members
    core = d % 2
    chip = d // 2
    chips = n_head // 2
    partner = 2 * chip + 1 - core
    per = rows // LANES
    half = n_head // 2
    scaling = LANES ** -0.5
    greet(g, d, n_ctx, n_head)

    def send(src, dst, s_sem, r_sem, to):
        pltpu.make_async_remote_copy(
            src_ref=src,
            dst_ref=dst,
            send_sem=s_sem,
            recv_sem=r_sem,
            device_id=to,
            device_id_type=MESH,
        ).start()

    def held_pair(src, p, held):
        return (
            src.at[p // members, :, 0, pl.ds((p % members) * quarter, quarter), :],
            held.at[pl.ds(per_dev * d, per_dev)],
        )

    def send_held(n, src, held):
        def one(o, _):
            p = lax.rem(d + o, n_head)
            send(*held_pair(src, p, held), ss.at[n], rs.at[n], (g, p))
            return 0

        lax.fori_loop(1, n_head, one, 0)
        pltpu.make_async_copy(*held_pair(src, d, held), rs.at[n]).start()

    def held_left(n, held):
        await_bytes(held.at[pl.ds(0, per_dev * (n_head - 1))], ss.at[n])

    def send_rows(src, got, n, r_sem, to_core):
        def one(o, _):
            t = lax.rem(chip + o, chips)
            send(src.at[2 * t // members], got.at[d], ss.at[n], r_sem, (g, 2 * t + to_core))
            return 0

        lax.fori_loop(1, chips, one, 0)

        @pl.when(core == to_core)
        def _():
            pltpu.make_async_copy(src.at[h], got.at[d], r_sem).start()

        @pl.when(core != to_core)
        def _():
            send(src.at[h], got.at[d], ss.at[n], r_sem, (g, partner))

    def rows_left(got, n, to_core):
        await_bytes(got.at[pl.ds(0, chips - 1)], ss.at[n])

        @pl.when(core != to_core)
        def _():
            await_bytes(got.at[0], ss.at[n])

    def forward(got, n, to_core):
        @pl.when(core == to_core)
        def _():
            await_bytes(got, rs.at[n])
            send(got, got, ss.at[4], rs.at[n], (g, partner))

    def send_retained(n, held, packed, got):
        await_bytes(held, rs.at[n])

        def one(s, _):
            off = near_first(s, n_ctx)
            c = lax.rem(g + off, n_ctx)
            for k in range(cap):
                packed[c, k] = held[jnp.clip(ids[c, k], 0, per_dev * n_head - 1)]

            @pl.when(s > 0)
            def _():
                send(packed.at[c], got.at[g], ss.at[6 + n], rs_line.at[n, off], (c, d))

            @pl.when(s == 0)
            def _():
                pltpu.make_async_copy(packed.at[c], got.at[g], rs_line.at[n, off]).start()

            return 0

        lax.fori_loop(0, n_ctx, one, 0)

    send_held(0, keys, k_held)

    plan((n_ctx, members, per_dev * n_head, own, cap), lists, counts, *[plans.at[e] for e in range(3)])
    for e, place in enumerate((ids, thr, inv)):
        pltpu.make_async_copy(plans.at[e], place, local_sem.at[e]).start()
    for e, place in enumerate((ids, thr, inv)):
        pltpu.make_async_copy(plans.at[e], place, local_sem.at[e]).wait()

    held_left(0, k_held)
    send_rows(q, q_got, 2, rs_q.at[d // per], 0)
    send_retained(0, k_held, k_send, k_got)
    for e in range(n_head // members):
        product = do[e].astype(jnp.float32) * out8[e].astype(jnp.float32)
        dl_send[e] = jnp.sum(product.T, axis=0, keepdims=True)

    def send_delta(o, _):
        p = lax.rem(d + o, n_head)
        send(dl_send.at[p // members], dl_got.at[d], ss.at[5], rs.at[4], (g, p))
        return 0

    lax.fori_loop(1, n_head, send_delta, 0)
    pltpu.make_async_copy(dl_send.at[h], dl_got.at[d], rs.at[4]).start()
    rows_left(q_got, 2, 0)
    send_held(1, vals, v_held)

    @pl.when(core == 0)
    def _():
        for i in range(own):
            block = q_got.at[pl.ds(i * per, per)]
            await_bytes(block, rs_q.at[i])
            send(block, block, ss.at[4], rs_q.at[i], (g, partner))

    send_rows(do, do_got, 3, rs.at[3], 1)

    def more():
        send_retained(1, v_held, v_send, v_got)

    gap = reach(rows, quarter, m)
    stats[...] = jnp.where(iota(stats.shape, 0) < 4, NEG, 0.0)

    def weigh(s, _):
        off = near_first(s, n_ctx)
        c = lax.rem(g - off + n_ctx, n_ctx)
        await_bytes(k_got.at[c], rs_line.at[0, off])

        @pl.when(s == HOOK)
        def _():
            more()

        for i in range(own):

            @pl.when((s == 0) & (core == 1))
            def _(i=i):
                await_bytes(q_got.at[pl.ds(i * per, per)], rs_q.at[i])

            key = k_got[c].reshape(cap * quarter, LANES)
            query = q_got[pl.ds(i * per, per)].reshape(rows, LANES)
            score = scaled(thr, i, c, n_ctx, cap, quarter, gap, nt(key, query))
            old = stats[pl.ds(i, 1)]
            new = jnp.maximum(old, jnp.max(score, axis=0, keepdims=True))
            weight = jnp.exp2(score - new)
            weights[c, i] = weight
            tops[c, pl.ds(i, 1)] = new
            stats[pl.ds(i, 1)] = new
            stats[pl.ds(4 + i, 1)] = stats[pl.ds(4 + i, 1)] * jnp.exp2(old - new) + jnp.sum(
                weight, axis=0, keepdims=True
            )
        return 0

    lax.fori_loop(0, n_ctx, weigh, 0)

    for o in range(1, members):
        to = (g, h * members + lax.rem(m + o, members))
        send(stats, shared.at[m], ss.at[8], rs.at[5], to)
    pltpu.make_async_copy(stats, shared.at[m], rs.at[5]).start()
    keys_t[...] = k_got[...].reshape(n_ctx * cap * quarter, LANES).T
    await_bytes(dl_got, rs.at[4])
    for i in range(own):
        delta[i : i + 1] = jnp.concatenate([dl_got[i * per + e] for e in range(per)], axis=1)
    forward(do_got, 3, 1)
    await_bytes(shared, rs.at[5])
    for i in range(own):
        each = [shared[e, i : i + 1] for e in range(members)]
        top = functools.reduce(jnp.maximum, each)
        mass = sum(shared[e, 4 + i : 5 + i] * jnp.exp2(each[e] - top) for e in range(members))
        lse[i : i + 1] = top + jnp.log2(mass)

    @pl.when(core == 0)
    def _():
        await_bytes(do_got, rs.at[3])

    def probs(c, i):
        return weights[c, i] * jnp.exp2(tops[c, pl.ds(i, 1)] - lse[pl.ds(i, 1)])

    def send_back(n, s, off, c, packed, back):
        place = back.at[g, pl.ds(0, cap)]

        @pl.when(s < n_ctx - 1)
        def _():
            send(packed.at[c], place, ss.at[9 + n], rs_line.at[2 + n, off], (c, d))

        @pl.when(s == n_ctx - 1)
        def _():
            pltpu.make_async_copy(packed.at[c], place, rs_line.at[2 + n, off]).start()

    zero = jnp.zeros((cap * quarter, LANES), jnp.float32)
    shape = (cap, quarter, LANES)

    def value_grads(s, _):
        off = far_first(s, n_ctx)
        c = lax.rem(g + off, n_ctx)

        acc = zero
        for i in range(own):
            cot = do_got[pl.ds(i * per, per)].reshape(rows, LANES)
            acc = acc + nn(probs(c, i).astype(jnp.bfloat16), cot)
        gv_send[c] = acc.astype(gv_send.dtype).reshape(shape)
        send_back(1, s, off, c, gv_send, v_back)
        return 0

    lax.fori_loop(0, n_ctx, value_grads, 0)

    for c in range(n_ctx):
        k_back[c, cap] = jnp.zeros(k_back.shape[2:], k_back.dtype)
        v_back[c, cap] = jnp.zeros(v_back.shape[2:], v_back.dtype)

    def finish(n, packed, back, total, out):
        for off in range(n_ctx):
            await_bytes(packed.at[0], rs_line.at[2 + n, off])

        def one(o, _):
            p = lax.rem(d + o, n_head)
            for e in range(per_dev):
                l = per_dev * p + e
                acc = back[0, jnp.clip(inv[0, l], 0, cap)].astype(jnp.float32)
                for c in range(1, n_ctx):
                    acc = acc + back[c, jnp.clip(inv[c, l], 0, cap)].astype(jnp.float32)
                total[l] = acc.astype(total.dtype)
            src = total.at[pl.ds(per_dev * p, per_dev)]
            place = out.at[h, :, 0, pl.ds(m * quarter, quarter), :]

            @pl.when(o < n_head)
            def _():
                send(src, place, ss.at[12 + n], rs.at[8 + n], (g, p))

            @pl.when(o == n_head)
            def _():
                pltpu.make_async_copy(src, place, rs.at[8 + n]).start()

            return 0

        lax.fori_loop(1, n_head + 1, one, 0)

    few = per // 2
    both = own // 2

    def exchange(side):
        for i in range(both * side, both * side + both):
            ds_all = ds_held[i - both * side].reshape(n_ctx * cap * quarter, rows)
            gq_full[i] = (nn(keys_t[...], ds_all).T * scaling).reshape(per, LANES, LANES)
            theirs = pl.ds(few * (1 - core), few)
            place = gq_send.at[pl.ds(i * per + few * (1 - core), few)]
            place[...] = gq_full[i, theirs].astype(gq_send.dtype)
            send(place, gq_pair.at[i], ss.at[11], rs.at[6 + 4 * side], (g, partner))

    def combine(side):
        await_bytes(gq_pair.at[pl.ds(both * side, both)], rs.at[6 + 4 * side])
        for i in range(both * side, both * side + both):
            part = gq_full[i, pl.ds(few * core, few)] + gq_pair[i].astype(jnp.float32)
            gq_send[pl.ds(i * per + few * core, few)] = part.astype(gq_send.dtype)
            for j in range(few):
                p = i * per + few * core + j

                @pl.when(p != d)
                def _(p=p):
                    send(gq_send.at[p], gq_got.at[chip], ss.at[14], rs.at[7], (g, p))

                @pl.when(p == d)
                def _(p=p):
                    pltpu.make_async_copy(gq_send.at[p], gq_got.at[chip], rs.at[7]).start()

    def key_part(c, side, acc):
        value = v_got[c].reshape(cap * quarter, LANES)
        for i in range(both * side, both * side + both):
            query = q_got[pl.ds(i * per, per)].reshape(rows, LANES)
            cot = do_got[pl.ds(i * per, per)].reshape(rows, LANES)
            dscore = (probs(c, i) * (nt(value, cot) - delta[pl.ds(i, 1)])).astype(jnp.bfloat16)
            ds_held[i - both * side, c] = dscore
            acc = acc + nn(dscore, query)
        return acc

    def first_side(s, _):
        off = near_first(s, n_ctx)
        c = lax.rem(g - off + n_ctx, n_ctx)
        await_bytes(v_got.at[c], rs_line.at[1, off])
        gk_acc[c] = key_part(c, 0, zero)
        return 0

    lax.fori_loop(0, n_ctx, first_side, 0)
    exchange(0)

    def second_side(s, _):
        off = far_first(s, n_ctx)
        c = lax.rem(g + off, n_ctx)

        @pl.when(s == HOOK_GQ)
        def _():
            combine(0)

        @pl.when(s == HOOK_SUM)
        def _():
            finish(1, gv_send, v_back, v_sum, gv_out)

        acc = key_part(c, 1, gk_acc[c])
        gk_send[c] = (acc * scaling).astype(gk_send.dtype).reshape(shape)
        send_back(0, s, off, c, gk_send, k_back)
        return 0

    lax.fori_loop(0, n_ctx, second_side, 0)
    exchange(1)
    combine(1)
    finish(0, gk_send, k_back, k_sum, gk_out)

    await_bytes(gq_got, rs.at[7])
    pair = members // 2

    def add_q(e, _):
        acc = gq_got[pair * e].astype(jnp.float32)
        for o in range(1, pair):
            acc = acc + gq_got[pair * e + o].astype(jnp.float32)
        gq_out[e] = acc.astype(gq_out.dtype)
        return 0

    lax.fori_loop(0, n_head // members, add_q, 0)
    await_bytes(k_sum, rs.at[8])
    await_bytes(v_sum, rs.at[9])
    held_left(1, v_held)
    rows_left(do_got, 3, 1)
    await_bytes(q_got, ss.at[4])
    await_bytes(dl_got.at[pl.ds(0, n_head - 1)], ss.at[5])
    for n, ref in ((6, k_send), (7, v_send), (9, gk_send), (10, gv_send)):
        await_bytes(ref.at[pl.ds(0, n_ctx - 1)], ss.at[n])
    await_bytes(shared.at[pl.ds(0, members - 1)], ss.at[8])
    await_bytes(gq_pair, ss.at[11])
    for n, ref in ((12, k_sum), (13, v_sum)):
        await_bytes(ref.at[pl.ds(0, per_dev * (n_head - 1))], ss.at[n])
    await_bytes(gq_send.at[pl.ds(0, half - 1)], ss.at[14])

    @pl.when((d % per) // few != core)
    def _():
        await_bytes(gq_send.at[0], ss.at[14])


def body(queries, keys, values, outputs, grad_out, block_ids, block_counts):
    f32, bf16, i32 = jnp.float32, jnp.bfloat16, jnp.int32
    n_ctx = lax.axis_size("ctx")
    n_head = lax.axis_size("head")
    kv, per_dev, _, blk, dh = keys.shape
    tokens, heads, _ = queries.shape
    members = n_head // kv
    quarter = blk // members
    group = heads // kv
    per_group = per_dev * n_head
    blocks, _, slots = block_ids.shape
    own = blocks // n_ctx
    cap = (slots + own + n_ctx - 2) // n_ctx
    part = tokens * group
    rows = blk * group
    any_ = whole(pl.ANY)
    vm = whole(VMEM)
    sm = whole(SMEM)
    limit = 60 * 2**20

    def by_kv(x):
        return jnp.transpose(x.reshape(tokens, kv, group, dh), (1, 0, 2, 3)).reshape(kv, part, dh)

    q8 = by_kv(queries)
    do8 = by_kv(grad_out)

    o8 = by_kv(outputs)
    packed = (n_ctx, cap, quarter, dh)
    back = (n_ctx, cap + 1, quarter, dh)
    held = (per_group, quarter, dh)
    spread = (n_head, part, dh)
    halves = (n_head // 2, part, dh)
    gq8, grad_keys, grad_values = pl.pallas_call(
        functools.partial(
            main_kernel, (n_ctx, n_head, members, per_dev, quarter, cap, own, rows)
        ),
        out_shape=[
            jax.ShapeDtypeStruct((kv, part, dh), bf16),
            jax.ShapeDtypeStruct(keys.shape, bf16),
            jax.ShapeDtypeStruct(keys.shape, bf16),
        ],
        in_specs=[vm] * 5 + [any_] * 2,
        out_specs=[vm, any_, any_],
        scratch_shapes=[
            VMEM((3, 8, LANES), i32),
            SMEM((8, LANES), i32),
            SMEM((8, LANES), i32),
            SMEM((8, LANES), i32),
            VMEM((kv, 1, part), f32),
            VMEM(held, bf16),
            VMEM(held, bf16),
            VMEM(packed, bf16),
            VMEM(packed, bf16),
            VMEM(packed, bf16),
            VMEM(packed, bf16),
            VMEM(spread, bf16),
            VMEM(spread, bf16),
            VMEM((n_head, 1, part), f32),
            VMEM((n_ctx, own, cap * quarter, rows), f32),
            VMEM((n_ctx, own, rows), f32),
            VMEM((8, rows), f32),
            VMEM((members, 8, rows), f32),
            VMEM((own, rows), f32),
            VMEM((own, rows), f32),
            VMEM((dh, n_ctx * cap * quarter), bf16),
            VMEM((own // 2, n_ctx, cap * quarter, rows), bf16),
            VMEM(spread, bf16),
            VMEM((own, rows // LANES, LANES, dh), f32),
            VMEM((n_ctx, cap * quarter, dh), f32),
            VMEM((own, rows // LANES // 2, LANES, dh), bf16),
            VMEM(halves, bf16),
            VMEM(packed, bf16),
            VMEM(packed, bf16),
            VMEM(back, bf16),
            VMEM(back, bf16),
            VMEM(held, bf16),
            VMEM(held, bf16),
            pltpu.SemaphoreType.DMA((15,)),
            pltpu.SemaphoreType.DMA((11,)),
            pltpu.SemaphoreType.DMA((4, n_ctx)),
            pltpu.SemaphoreType.DMA((own,)),
            pltpu.SemaphoreType.DMA((3,)),
        ],
        compiler_params=pltpu.CompilerParams(
            collective_id=0, has_side_effects=True, vmem_limit_bytes=limit
        ),
        name="main",
    )(block_ids, block_counts.T, q8, do8, o8, keys, values)
    grad_queries = jnp.transpose(gq8.reshape(kv, tokens, group, dh), (1, 0, 2, 3)).reshape(
        tokens, heads, dh
    )
    return grad_queries, grad_keys, grad_values


def solution(mesh):
    tok = P(("ctx", "head"), None, None)
    cached = P(None, "head", "ctx", None, None)
    return jax.shard_map(
        body,
        mesh=mesh,
        in_specs=(tok, cached, cached, tok, tok, P(), P()),
        out_specs=(tok, cached, cached),
        check_vma=False,
    )
```

```python
import functools

import jax
import jax.numpy as jnp
from jax import lax
from jax.experimental import pallas as pl
from jax.experimental.pallas import tpu as pltpu
from jax.sharding import PartitionSpec as P

MESH = pl.DeviceIdType.MESH
VMEM = pltpu.VMEM
SMEM = pltpu.SMEM
NEG = -1e30
LOG2E = 1.4426950408889634
LANES = 128
FAR = 4096
HOOK = 5
HOOK_SUM = 3
HOOK_GQ = 1


def whole(space):
    return pl.BlockSpec(memory_space=space)


def nt(a, b):
    return lax.dot_general(a, b, (((1,), (1,)), ((), ())), preferred_element_type=jnp.float32)


def nn(a, b):
    return lax.dot_general(a, b, (((1,), (0,)), ((), ())), preferred_element_type=jnp.float32)


def iota(shape, dim):
    return lax.broadcasted_iota(jnp.int32, shape, dim)


def plan(dims, lists_ref, counts_ref, ids_ref, thr_ref, inv_ref):
    n_ctx, members, per_group, own, cap = dims
    g = lax.axis_index("ctx")
    h = lax.axis_index("head") // members
    blocks, kv, slots = lists_ref.shape
    total = n_ctx * per_group
    pick = iota((blocks, kv, slots), 1) == h
    lists = jnp.sum(jnp.where(pick, lists_ref[...].astype(jnp.float32), 0.0), axis=1)
    count = jnp.sum(
        jnp.where(iota((kv, blocks), 0) == h, counts_ref[...].astype(jnp.float32), 0.0),
        axis=0,
        keepdims=True,
    )
    square = iota((blocks, blocks), 0) == iota((blocks, blocks), 1)
    count = jnp.sum(jnp.where(square, count, 0.0), axis=1, keepdims=True)
    lists = jnp.where(iota((blocks, slots), 1).astype(jnp.float32) < count, lists, -1.0)
    col = iota((1, total), 1)
    col_id = ((col % per_group) * n_ctx + col // per_group).astype(jnp.float32)
    live = jnp.zeros((blocks, total), jnp.float32)
    for n in range(slots):
        live = jnp.where(lists[:, n : n + 1] == col_id, 1.0, live)
    low = live.astype(jnp.bfloat16)
    of_group = (iota((8, blocks), 1) // own == iota((8, blocks), 0)).astype(jnp.float32)
    used = nn(of_group.astype(jnp.bfloat16), low) > 0.5
    used_f = used.astype(jnp.float32)
    before = (iota((total, total), 0) // per_group == iota((total, total), 1) // per_group) & (
        iota((total, total), 0) < iota((total, total), 1)
    )
    place = nn(used_f.astype(jnp.bfloat16), before.astype(jnp.float32).astype(jnp.bfloat16))
    rows8 = iota((8, blocks), 0)
    own_rows = ((iota((8, blocks), 1) == own * g + rows8) & (rows8 < own)).astype(jnp.float32)
    own_live = nn(own_rows.astype(jnp.bfloat16), low)
    row8 = iota((8, total), 0)
    diag = (
        (col_id == (total - blocks + own * g + row8).astype(jnp.float32)) & (row8 < own)
    ).astype(jnp.float32)
    key_row = iota((total, 2 * LANES), 0)
    lane = iota((total, 2 * LANES), 1)
    key_group = key_row // per_group
    key_local = key_row % per_group
    got = jnp.zeros((24, 2 * LANES), jnp.float32)
    for k in range(cap):
        match = jnp.where(used & (place == k), 1.0, 0.0)
        mine = jnp.sum(jnp.where(row8 == g, match, 0.0), axis=0, keepdims=True)
        left = jnp.concatenate([match, own_live * mine, diag * mine], axis=0)
        right = jnp.where(
            lane == k,
            jnp.where(key_group == g, key_local, 0),
            jnp.where(lane == LANES + k * n_ctx + key_group, 1, 0),
        )
        got = got + nn(left.astype(jnp.bfloat16), right.astype(jnp.float32).astype(jnp.bfloat16))
    ids_ref[...] = got[0:8, :LANES].astype(jnp.int32)
    is_live = got[8:16, LANES:] > 0.5
    is_diag = got[16:24, LANES:] > 0.5
    thr_ref[...] = jnp.where(is_diag & is_live, 0, jnp.where(is_live, -FAR, FAR))
    held_at = ((iota((total, LANES), 0) // per_group == g)
               & (iota((total, LANES), 0) % per_group == iota((total, LANES), 1)))
    back = nn(
        jnp.where(used, place, float(cap)).astype(jnp.bfloat16),
        held_at.astype(jnp.float32).astype(jnp.bfloat16),
    )
    inv_ref[...] = back.astype(jnp.int32)


def greet(g, d, n_ctx, n_head):
    barrier = pltpu.get_barrier_semaphore()

    def plane(o, _):
        pl.semaphore_signal(
            barrier, inc=1, device_id=(g, lax.rem(d + o, n_head)), device_id_type=MESH
        )
        return 0

    lax.fori_loop(1, n_head, plane, 0)

    def line(o, _):
        pl.semaphore_signal(
            barrier, inc=1, device_id=(lax.rem(g + o, n_ctx), d), device_id_type=MESH
        )
        return 0

    lax.fori_loop(1, n_ctx, line, 0)
    pl.semaphore_wait(barrier, n_head + n_ctx - 2)


def await_bytes(ref, sem):
    pltpu.make_async_copy(ref, ref, sem).wait()


def near_first(s, n):
    return lax.rem((s % 2) * ((s + 1) // 2) + (1 - s % 2) * (n - s // 2), n)


def far_first(s, n):
    return n // 2 + ((s + 1) // 2) * (1 - 2 * (s % 2))


def reach(rows, quarter, m):
    shape = (quarter, rows)
    return iota(shape, 1) // 8 - iota(shape, 0) - m * quarter


def scaled(thr, i, c, n_ctx, cap, quarter, gap, raw):
    factor = (LANES ** -0.5) * LOG2E
    parts = []
    for k in range(cap):
        part = raw[k * quarter : (k + 1) * quarter] * factor
        parts.append(jnp.where(gap >= thr[i, k * n_ctx + c], part, NEG))
    return jnp.concatenate(parts, axis=0)


def main_kernel(
    dims,
    lists,
    counts,
    q,
    do,
    out8,
    keys,
    vals,
    gq_out,
    gk_out,
    gv_out,
    plans,
    ids,
    thr,
    inv,
    dl_send,
    k_held,
    v_held,
    k_send,
    v_send,
    k_got,
    v_got,
    q_got,
    do_got,
    dl_got,
    weights,
    tops,
    stats,
    shared,
    lse,
    delta,
    keys_t,
    ds_held,
    gq_send,
    gq_full,
    gk_acc,
    gq_pair,
    gq_got,
    gk_send,
    gv_send,
    k_back,
    v_back,
    k_sum,
    v_sum,
    ss,
    rs,
    rs_line,
    rs_q,
    local_sem,
):
    n_ctx, n_head, members, per_dev, quarter, cap, own, rows = dims
    g = lax.axis_index("ctx")
    d = lax.axis_index("head")
    h = d // members
    m = d % members
    core = d % 2
    chip = d // 2
    chips = n_head // 2
    partner = 2 * chip + 1 - core
    per = rows // LANES
    half = n_head // 2
    scaling = LANES ** -0.5
    greet(g, d, n_ctx, n_head)

    def send(src, dst, s_sem, r_sem, to):
        pltpu.make_async_remote_copy(
            src_ref=src,
            dst_ref=dst,
            send_sem=s_sem,
            recv_sem=r_sem,
            device_id=to,
            device_id_type=MESH,
        ).start()

    def held_pair(src, p, held):
        return (
            src.at[p // members, :, 0, pl.ds((p % members) * quarter, quarter), :],
            held.at[pl.ds(per_dev * d, per_dev)],
        )

    def send_held(n, src, held):
        def one(o, _):
            p = lax.rem(d + o, n_head)
            send(*held_pair(src, p, held), ss.at[n], rs.at[n], (g, p))
            return 0

        lax.fori_loop(1, n_head, one, 0)
        pltpu.make_async_copy(*held_pair(src, d, held), rs.at[n]).start()

    def held_left(n, held):
        await_bytes(held.at[pl.ds(0, per_dev * (n_head - 1))], ss.at[n])

    def send_rows(src, got, n, r_sem, to_core):
        def one(o, _):
            t = lax.rem(chip + o, chips)
            send(src.at[2 * t // members], got.at[d], ss.at[n], r_sem, (g, 2 * t + to_core))
            return 0

        lax.fori_loop(1, chips, one, 0)

        @pl.when(core == to_core)
        def _():
            pltpu.make_async_copy(src.at[h], got.at[d], r_sem).start()

        @pl.when(core != to_core)
        def _():
            send(src.at[h], got.at[d], ss.at[n], r_sem, (g, partner))

    def rows_left(got, n, to_core):
        await_bytes(got.at[pl.ds(0, chips - 1)], ss.at[n])

        @pl.when(core != to_core)
        def _():
            await_bytes(got.at[0], ss.at[n])

    def forward(got, n, to_core):
        @pl.when(core == to_core)
        def _():
            await_bytes(got, rs.at[n])
            send(got, got, ss.at[4], rs.at[n], (g, partner))

    def send_retained(n, held, packed, got):
        await_bytes(held, rs.at[n])

        def one(s, _):
            off = near_first(s, n_ctx)
            c = lax.rem(g + off, n_ctx)
            for k in range(cap):
                packed[c, k] = held[jnp.clip(ids[c, k], 0, per_dev * n_head - 1)]

            @pl.when(s > 0)
            def _():
                send(packed.at[c], got.at[g], ss.at[6 + n], rs_line.at[n, off], (c, d))

            @pl.when(s == 0)
            def _():
                pltpu.make_async_copy(packed.at[c], got.at[g], rs_line.at[n, off]).start()

            return 0

        lax.fori_loop(0, n_ctx, one, 0)

    send_held(0, keys, k_held)

    plan((n_ctx, members, per_dev * n_head, own, cap), lists, counts, *[plans.at[e] for e in range(3)])
    for e, place in enumerate((ids, thr, inv)):
        pltpu.make_async_copy(plans.at[e], place, local_sem.at[e]).start()
    for e, place in enumerate((ids, thr, inv)):
        pltpu.make_async_copy(plans.at[e], place, local_sem.at[e]).wait()

    held_left(0, k_held)
    send_rows(q, q_got, 2, rs_q.at[d // per], 0)
    send_retained(0, k_held, k_send, k_got)
    for e in range(n_head // members):
        product = do[e].astype(jnp.float32) * out8[e].astype(jnp.float32)
        dl_send[e] = jnp.sum(product.T, axis=0, keepdims=True)

    def send_delta(o, _):
        p = lax.rem(d + o, n_head)
        send(dl_send.at[p // members], dl_got.at[d], ss.at[5], rs.at[4], (g, p))
        return 0

    lax.fori_loop(1, n_head, send_delta, 0)
    pltpu.make_async_copy(dl_send.at[h], dl_got.at[d], rs.at[4]).start()
    rows_left(q_got, 2, 0)
    send_held(1, vals, v_held)

    @pl.when(core == 0)
    def _():
        for i in range(own):
            block = q_got.at[pl.ds(i * per, per)]
            await_bytes(block, rs_q.at[i])
            send(block, block, ss.at[4], rs_q.at[i], (g, partner))

    send_rows(do, do_got, 3, rs.at[3], 1)

    def more():
        send_retained(1, v_held, v_send, v_got)

    gap = reach(rows, quarter, m)
    stats[...] = jnp.where(iota(stats.shape, 0) < 4, NEG, 0.0)

    def weigh(s, _):
        off = near_first(s, n_ctx)
        c = lax.rem(g - off + n_ctx, n_ctx)
        await_bytes(k_got.at[c], rs_line.at[0, off])

        @pl.when(s == HOOK)
        def _():
            more()

        for i in range(own):

            @pl.when((s == 0) & (core == 1))
            def _(i=i):
                await_bytes(q_got.at[pl.ds(i * per, per)], rs_q.at[i])

            key = k_got[c].reshape(cap * quarter, LANES)
            query = q_got[pl.ds(i * per, per)].reshape(rows, LANES)
            score = scaled(thr, i, c, n_ctx, cap, quarter, gap, nt(key, query))
            old = stats[pl.ds(i, 1)]
            new = jnp.maximum(old, jnp.max(score, axis=0, keepdims=True))
            weight = jnp.exp2(score - new)
            weights[c, i] = weight
            tops[c, pl.ds(i, 1)] = new
            stats[pl.ds(i, 1)] = new
            stats[pl.ds(4 + i, 1)] = stats[pl.ds(4 + i, 1)] * jnp.exp2(old - new) + jnp.sum(
                weight, axis=0, keepdims=True
            )
        return 0

    lax.fori_loop(0, n_ctx, weigh, 0)

    for o in range(1, members):
        to = (g, h * members + lax.rem(m + o, members))
        send(stats, shared.at[m], ss.at[8], rs.at[5], to)
    pltpu.make_async_copy(stats, shared.at[m], rs.at[5]).start()
    keys_t[...] = k_got[...].reshape(n_ctx * cap * quarter, LANES).T
    await_bytes(dl_got, rs.at[4])
    for i in range(own):
        delta[i : i + 1] = jnp.concatenate([dl_got[i * per + e] for e in range(per)], axis=1)
    forward(do_got, 3, 1)
    await_bytes(shared, rs.at[5])
    for i in range(own):
        each = [shared[e, i : i + 1] for e in range(members)]
        top = functools.reduce(jnp.maximum, each)
        mass = sum(shared[e, 4 + i : 5 + i] * jnp.exp2(each[e] - top) for e in range(members))
        lse[i : i + 1] = top + jnp.log2(mass)

    @pl.when(core == 0)
    def _():
        await_bytes(do_got, rs.at[3])

    def probs(c, i):
        return weights[c, i] * jnp.exp2(tops[c, pl.ds(i, 1)] - lse[pl.ds(i, 1)])

    def send_back(n, s, off, c, packed, back):
        place = back.at[g, pl.ds(0, cap)]

        @pl.when(s < n_ctx - 1)
        def _():
            send(packed.at[c], place, ss.at[9 + n], rs_line.at[2 + n, off], (c, d))

        @pl.when(s == n_ctx - 1)
        def _():
            pltpu.make_async_copy(packed.at[c], place, rs_line.at[2 + n, off]).start()

    zero = jnp.zeros((cap * quarter, LANES), jnp.float32)
    shape = (cap, quarter, LANES)

    def value_grads(s, _):
        off = far_first(s, n_ctx)
        c = lax.rem(g + off, n_ctx)

        acc = zero
        for i in range(own):
            cot = do_got[pl.ds(i * per, per)].reshape(rows, LANES)
            acc = acc + nn(probs(c, i).astype(jnp.bfloat16), cot)
        gv_send[c] = acc.astype(gv_send.dtype).reshape(shape)
        send_back(1, s, off, c, gv_send, v_back)
        return 0

    lax.fori_loop(0, n_ctx, value_grads, 0)

    for c in range(n_ctx):
        k_back[c, cap] = jnp.zeros(k_back.shape[2:], k_back.dtype)
        v_back[c, cap] = jnp.zeros(v_back.shape[2:], v_back.dtype)

    def finish(n, packed, back, total, out):
        for off in range(n_ctx):
            await_bytes(packed.at[0], rs_line.at[2 + n, off])

        def one(o, _):
            p = lax.rem(d + o, n_head)
            for e in range(per_dev):
                l = per_dev * p + e
                acc = back[0, jnp.clip(inv[0, l], 0, cap)].astype(jnp.float32)
                for c in range(1, n_ctx):
                    acc = acc + back[c, jnp.clip(inv[c, l], 0, cap)].astype(jnp.float32)
                total[l] = acc.astype(total.dtype)
            src = total.at[pl.ds(per_dev * p, per_dev)]
            place = out.at[h, :, 0, pl.ds(m * quarter, quarter), :]

            @pl.when(o < n_head)
            def _():
                send(src, place, ss.at[12 + n], rs.at[8 + n], (g, p))

            @pl.when(o == n_head)
            def _():
                pltpu.make_async_copy(src, place, rs.at[8 + n]).start()

            return 0

        lax.fori_loop(1, n_head + 1, one, 0)

    few = per // 2
    both = own // 2

    def exchange(side):
        for i in range(both * side, both * side + both):
            ds_all = ds_held[i - both * side].reshape(n_ctx * cap * quarter, rows)
            gq_full[i] = (nn(keys_t[...], ds_all).T * scaling).reshape(per, LANES, LANES)
            theirs = pl.ds(few * (1 - core), few)
            place = gq_send.at[pl.ds(i * per + few * (1 - core), few)]
            place[...] = gq_full[i, theirs].astype(gq_send.dtype)
            send(place, gq_pair.at[i], ss.at[11], rs.at[6 + 4 * side], (g, partner))

    def combine(side):
        await_bytes(gq_pair.at[pl.ds(both * side, both)], rs.at[6 + 4 * side])
        for i in range(both * side, both * side + both):
            part = gq_full[i, pl.ds(few * core, few)] + gq_pair[i].astype(jnp.float32)
            gq_send[pl.ds(i * per + few * core, few)] = part.astype(gq_send.dtype)
            for j in range(few):
                p = i * per + few * core + j

                @pl.when(p != d)
                def _(p=p):
                    send(gq_send.at[p], gq_got.at[chip], ss.at[14], rs.at[7], (g, p))

                @pl.when(p == d)
                def _(p=p):
                    pltpu.make_async_copy(gq_send.at[p], gq_got.at[chip], rs.at[7]).start()

    def key_part(c, side, acc):
        value = v_got[c].reshape(cap * quarter, LANES)
        for i in range(both * side, both * side + both):
            query = q_got[pl.ds(i * per, per)].reshape(rows, LANES)
            cot = do_got[pl.ds(i * per, per)].reshape(rows, LANES)
            dscore = (probs(c, i) * (nt(value, cot) - delta[pl.ds(i, 1)])).astype(jnp.bfloat16)
            ds_held[i - both * side, c] = dscore
            acc = acc + nn(dscore, query)
        return acc

    def first_side(s, _):
        off = near_first(s, n_ctx)
        c = lax.rem(g - off + n_ctx, n_ctx)
        await_bytes(v_got.at[c], rs_line.at[1, off])
        gk_acc[c] = key_part(c, 0, zero)
        return 0

    lax.fori_loop(0, n_ctx, first_side, 0)
    exchange(0)

    def second_side(s, _):
        off = far_first(s, n_ctx)
        c = lax.rem(g + off, n_ctx)

        @pl.when(s == HOOK_GQ)
        def _():
            combine(0)

        @pl.when(s == HOOK_SUM)
        def _():
            finish(1, gv_send, v_back, v_sum, gv_out)

        acc = key_part(c, 1, gk_acc[c])
        gk_send[c] = (acc * scaling).astype(gk_send.dtype).reshape(shape)
        send_back(0, s, off, c, gk_send, k_back)
        return 0

    lax.fori_loop(0, n_ctx, second_side, 0)
    exchange(1)
    combine(1)
    finish(0, gk_send, k_back, k_sum, gk_out)

    await_bytes(gq_got, rs.at[7])
    pair = members // 2

    def add_q(e, _):
        acc = gq_got[pair * e].astype(jnp.float32)
        for o in range(1, pair):
            acc = acc + gq_got[pair * e + o].astype(jnp.float32)
        gq_out[e] = acc.astype(gq_out.dtype)
        return 0

    lax.fori_loop(0, n_head // members, add_q, 0)
    await_bytes(k_sum, rs.at[8])
    await_bytes(v_sum, rs.at[9])
    held_left(1, v_held)
    rows_left(do_got, 3, 1)
    await_bytes(q_got, ss.at[4])
    await_bytes(dl_got.at[pl.ds(0, n_head - 1)], ss.at[5])
    for n, ref in ((6, k_send), (7, v_send), (9, gk_send), (10, gv_send)):
        await_bytes(ref.at[pl.ds(0, n_ctx - 1)], ss.at[n])
    await_bytes(shared.at[pl.ds(0, members - 1)], ss.at[8])
    await_bytes(gq_pair, ss.at[11])
    for n, ref in ((12, k_sum), (13, v_sum)):
        await_bytes(ref.at[pl.ds(0, per_dev * (n_head - 1))], ss.at[n])
    await_bytes(gq_send.at[pl.ds(0, half - 1)], ss.at[14])

    @pl.when((d % per) // few != core)
    def _():
        await_bytes(gq_send.at[0], ss.at[14])


def body(queries, keys, values, outputs, grad_out, block_ids, block_counts):
    f32, bf16, i32 = jnp.float32, jnp.bfloat16, jnp.int32
    n_ctx = lax.axis_size("ctx")
    n_head = lax.axis_size("head")
    kv, per_dev, _, blk, dh = keys.shape
    tokens, heads, _ = queries.shape
    members = n_head // kv
    quarter = blk // members
    group = heads // kv
    per_group = per_dev * n_head
    blocks, _, slots = block_ids.shape
    own = blocks // n_ctx
    cap = (slots + own + n_ctx - 2) // n_ctx
    part = tokens * group
    rows = blk * group
    any_ = whole(pl.ANY)
    vm = whole(VMEM)
    sm = whole(SMEM)
    limit = 60 * 2**20

    def by_kv(x):
        return jnp.transpose(x.reshape(tokens, kv, group, dh), (1, 0, 2, 3)).reshape(kv, part, dh)

    q8 = by_kv(queries)
    do8 = by_kv(grad_out)

    o8 = by_kv(outputs)
    packed = (n_ctx, cap, quarter, dh)
    back = (n_ctx, cap + 1, quarter, dh)
    held = (per_group, quarter, dh)
    spread = (n_head, part, dh)
    halves = (n_head // 2, part, dh)
    gq8, grad_keys, grad_values = pl.pallas_call(
        functools.partial(
            main_kernel, (n_ctx, n_head, members, per_dev, quarter, cap, own, rows)
        ),
        out_shape=[
            jax.ShapeDtypeStruct((kv, part, dh), bf16),
            jax.ShapeDtypeStruct(keys.shape, bf16),
            jax.ShapeDtypeStruct(keys.shape, bf16),
        ],
        in_specs=[vm] * 5 + [any_] * 2,
        out_specs=[vm, any_, any_],
        scratch_shapes=[
            VMEM((3, 8, LANES), i32),
            SMEM((8, LANES), i32),
            SMEM((8, LANES), i32),
            SMEM((8, LANES), i32),
            VMEM((kv, 1, part), f32),
            VMEM(held, bf16),
            VMEM(held, bf16),
            VMEM(packed, bf16),
            VMEM(packed, bf16),
            VMEM(packed, bf16),
            VMEM(packed, bf16),
            VMEM(spread, bf16),
            VMEM(spread, bf16),
            VMEM((n_head, 1, part), f32),
            VMEM((n_ctx, own, cap * quarter, rows), f32),
            VMEM((n_ctx, own, rows), f32),
            VMEM((8, rows), f32),
            VMEM((members, 8, rows), f32),
            VMEM((own, rows), f32),
            VMEM((own, rows), f32),
            VMEM((dh, n_ctx * cap * quarter), bf16),
            VMEM((own // 2, n_ctx, cap * quarter, rows), bf16),
            VMEM(spread, bf16),
            VMEM((own, rows // LANES, LANES, dh), f32),
            VMEM((n_ctx, cap * quarter, dh), f32),
            VMEM((own, rows // LANES // 2, LANES, dh), bf16),
            VMEM(halves, bf16),
            VMEM(packed, bf16),
            VMEM(packed, bf16),
            VMEM(back, bf16),
            VMEM(back, bf16),
            VMEM(held, bf16),
            VMEM(held, bf16),
            pltpu.SemaphoreType.DMA((15,)),
            pltpu.SemaphoreType.DMA((11,)),
            pltpu.SemaphoreType.DMA((4, n_ctx)),
            pltpu.SemaphoreType.DMA((own,)),
            pltpu.SemaphoreType.DMA((3,)),
        ],
        compiler_params=pltpu.CompilerParams(
            collective_id=0, has_side_effects=True, vmem_limit_bytes=limit
        ),
        name="main",
    )(block_ids, block_counts.T, q8, do8, o8, keys, values)
    grad_queries = jnp.transpose(gq8.reshape(kv, tokens, group, dh), (1, 0, 2, 3)).reshape(
        tokens, heads, dh
    )
    return grad_queries, grad_keys, grad_values


def solution(mesh):
    tok = P(("ctx", "head"), None, None)
    cached = P(None, "head", "ctx", None, None)
    return jax.shard_map(
        body,
        mesh=mesh,
        in_specs=(tok, cached, cached, tok, tok, P(), P()),
        out_specs=(tok, cached, cached),
        check_vma=False,
    )
```
